768 devices in a mesh: rows: 192 (over y, z, core), cols: 4 (over x).
Axes of the slice: x: 4, y: 8, z: 12, core: 2. Of those that a mesh axis runs over, the one named last changes fastest.
Arguments:
- features: bfloat16 [294912, 256], P(('rows', 'cols')), may hold values from -6 to 6
- pre_act: bfloat16 [294912, 256], P(('rows', 'cols')), may hold values from -6 to 6
- upstream: float32 [294912, 256], P(('rows', 'cols')), may hold values from -6 to 6
- weight: bfloat16 [256, 256], replicated, may hold values from -0.375 to 0.375
- tile_values: bfloat16 [55296, 128, 128], P(('rows', 'cols')), may hold values from -0.1875 to 0.1875
- tile_list: int32 [55296, 3], P(('rows', 'cols')), may hold values from 0 to 2303, as said below
- tile_counts: int32 [768], P(('rows', 'cols')), may hold values from 9 to 72, as said below
Outputs:
- grad_features: float32 [294912, 256], P(('rows', 'cols'))
- grad_weight: float32 [256, 256], replicated
The draws below stay inside these ranges and needn't reach their ends.
Inputs may be any that keep to these rules, and one draw needn't show every extreme that they name: `tile_list`: for slot d * 72 + k: column 0 is one of device d's own blocks; column 1 is a block owned by a device whose rows index differs from device d's rows index by at most one; column 2, over device d's 72 slots, takes every value 0 to 71 once. Slots that are not live hold valid entries too. `tile_counts`: some device has all 72 slots live.
All inputs are finite; a program needn't handle non-finite values.
Results may differ from the reference program's by a relative error of at most 0.0041.
Values may be sent and summed in bfloat16 or wider, within the bound.
No kernel may reach another device: no remote copies, remote signals or barrier semaphores. Data moves between devices by JAX's collectives and lax.ppermute only.
A program may use at most 128 MiB of HBM per device.

```python
import math
import jax
import jax.numpy as jnp
from jax import lax

F = 256
BLK = 128
NB = 3
TCAP = 72
NODES = 294912
N_ROWS = 192
N_COLS = 4


def shuffle_slots(subkey):
    return jax.random.permutation(subkey, TCAP)


def draw_tile_list(key, part):
    key = jax.random.fold_in(key, 11)
    subkeys = jax.random.split(key, 5)
    device_count = N_ROWS * N_COLS
    total_slots = device_count * TCAP
    slot_ids = jnp.arange(total_slots, dtype=jnp.int32)
    device_ids = slot_ids // TCAP
    device_row = device_ids // N_COLS
    dst_local = jax.random.randint(subkeys[0], (total_slots,), 0, NB)
    row_step = jax.random.randint(subkeys[1], (total_slots,), -1, 2)
    src_row = jnp.clip(device_row + row_step, 0, N_ROWS - 1)
    src_col = jax.random.randint(subkeys[2], (total_slots,), 0, N_COLS)
    src_local = jax.random.randint(subkeys[3], (total_slots,), 0, NB)
    src_block = (src_row * N_COLS + src_col) * NB + src_local
    src_block = jnp.where(slot_ids == 0, 0, src_block)
    src_block = jnp.where(slot_ids == total_slots - 1, device_count * NB - 1, src_block)
    orders = jax.vmap(shuffle_slots)(jax.random.split(subkeys[4], device_count)).reshape(-1)
    dst_block = device_ids * NB + dst_local
    return jnp.stack([dst_block, src_block, orders.astype(jnp.int32)], axis=1).astype(jnp.int32)


def draw_tile_counts(key, part):
    key = jax.random.fold_in(key, 12)
    subkeys = jax.random.split(key, 2)
    device_count = N_ROWS * N_COLS
    divisors = jax.random.randint(subkeys[0], (device_count,), 1, 9)
    counts = TCAP // divisors
    busiest = jax.random.randint(subkeys[1], (), 0, device_count)
    counts = jnp.where(jnp.arange(device_count) == busiest, TCAP, counts)
    return counts.astype(jnp.int32)


def block_levels(rng, shape, pieces, low, top_value):
    factor_of, own = 1.0, jax.random.fold_in(rng, 6)
    for position, blocks in pieces:
        steps = jnp.exp(jax.random.uniform(jax.random.fold_in(own, position), (blocks,), jnp.float32, low / len(pieces), top_value / len(pieces)))
        factor_of = factor_of * jnp.repeat(steps, shape[position] // blocks).reshape([-1 if axis == position else 1 for axis in range(len(shape))])
    return factor_of


def scatter_about(stream_key, shape, scale, most, cuts=(), held_as=jnp.bfloat16):
    entries = jax.random.normal(stream_key, shape, jnp.float32) * scale
    if len(cuts) > 0:
        entries = block_levels(stream_key, shape, cuts, -0.22, 0.18) * entries
    return jnp.clip(entries, min=-most, max=most).astype(held_as)


def setup_inputs(seed: int = 0) -> dict:
    arg_keys = jax.random.split(jax.random.key(seed), 8)
    features = scatter_about(arg_keys[0], (NODES, F), 1.0, 6.0, ((0, 768),))
    pre_act = scatter_about(arg_keys[1], (NODES, F), 1.0, 6.0, ((0, 768),))
    upstream = scatter_about(arg_keys[2], (NODES, F), 1.0, 6.0, ((0, 768),), jnp.float32)
    weight = scatter_about(arg_keys[3], (F, F), F ** -0.5, 0.375)
    tile_values = scatter_about(arg_keys[4], (N_ROWS * N_COLS * TCAP, BLK, BLK), (8 * BLK) ** -0.5, 0.1875, ((0, 768),))
    tile_list = draw_tile_list(jax.random.fold_in(arg_keys[7], 71), 0)
    tile_counts = draw_tile_counts(jax.random.fold_in(arg_keys[7], 71), 0)
    return dict(features=features, pre_act=pre_act, upstream=upstream, weight=weight, tile_values=tile_values, tile_list=tile_list, tile_counts=tile_counts)


def starts(*values):
    return tuple((jnp.asarray(value).astype(jnp.int32) for value in values))

def reference(features, pre_act, upstream, weight, tile_values, tile_list, tile_counts):
    device_count = N_ROWS * N_COLS
    rows_dev = NB * BLK
    row_rows = N_COLS * rows_dev
    row_blocks = N_COLS * NB
    node_count = device_count * rows_dev
    masked = jnp.where(pre_act > 0, upstream, 0.0).astype(jnp.bfloat16)
    back_grad = lax.dot_general(masked, weight, (((1,), (1,)), ((), ())), preferred_element_type=jnp.float32).astype(jnp.bfloat16)
    feat_pad = jnp.pad(features.astype(jnp.float32), ((row_rows, row_rows), (0, 0)))
    grad_pad = jnp.zeros((node_count + 2 * row_rows, F), jnp.float32)
    weight_acc = jnp.zeros((F, F), jnp.float32)
    slot_ids = jnp.arange(TCAP, dtype=jnp.int32)

    def device_step(state_pair, device):
        grad_acc, weight_sum = state_pair
        band_row = device // N_COLS
        band_start = band_row * row_rows
        band_rows = lax.dynamic_slice(feat_pad, starts(band_start, 0), (3 * row_rows, F)).reshape(3 * row_blocks, BLK, F)
        tile_rows = lax.dynamic_slice(tile_list, starts(device * TCAP, 0), (TCAP, 3))
        dev_tiles = lax.dynamic_slice(tile_values, starts(device * TCAP, 0, 0), (TCAP, BLK, BLK))
        tile_mats = jnp.take(dev_tiles, tile_rows[:, 2], axis=0).astype(jnp.float32)
        active = (slot_ids < tile_counts[device]).astype(jnp.float32)[:, None, None]
        dst_index = (tile_rows[:, 0] - device * NB).astype(jnp.int32)
        src_index = (tile_rows[:, 1] - (band_row - 1) * row_blocks).astype(jnp.int32)
        own_start = device * rows_dev
        dz_rows = lax.dynamic_slice(masked, starts(own_start, 0), (rows_dev, F)).astype(jnp.float32)
        dy_blocks = lax.dynamic_slice(back_grad, starts(own_start, 0), (rows_dev, F)).astype(jnp.float32).reshape(NB, BLK, F)
        sources = jnp.take(band_rows, src_index, axis=0)
        products = jnp.einsum('tij,tjf->tif', tile_mats, sources, precision=lax.Precision.HIGHEST) * active
        aggregate = jnp.zeros((NB, BLK, F), jnp.float32).at[dst_index].add(products)
        weight_sum = weight_sum + jnp.dot(aggregate.reshape(rows_dev, F).T, dz_rows, precision=lax.Precision.HIGHEST)
        contrib = jnp.einsum('tij,tif->tjf', tile_mats, jnp.take(dy_blocks, dst_index, axis=0), precision=lax.Precision.HIGHEST) * active
        contrib_slab = jnp.zeros((3 * row_blocks, BLK, F), jnp.float32).at[src_index].add(contrib).reshape(3 * row_rows, F)
        current = lax.dynamic_slice(grad_acc, starts(band_start, 0), (3 * row_rows, F))
        grad_acc = lax.dynamic_update_slice(grad_acc, current + contrib_slab, starts(band_start, 0))
        return ((grad_acc, weight_sum), None)
    final_pair, unused = lax.scan(device_step, (grad_pad, weight_acc), jnp.arange(device_count, dtype=jnp.int32))
    grad_features = final_pair[0][row_rows:row_rows + node_count]
    grad_weight = final_pair[1] / math.sqrt(node_count)
    return (grad_features, grad_weight)
```

```python
import functools
import math

import jax
import jax.numpy as jnp
from jax import lax
from jax.experimental import pallas as pl
from jax.experimental.pallas import tpu as pltpu
from jax.sharding import Mesh, PartitionSpec as P

GROUP = 8
VMEM = pl.BlockSpec(memory_space=pltpu.VMEM)
SMEM = pl.BlockSpec(memory_space=pltpu.SMEM)


def tile_kernel(base, count, slots, pre, up, tiles, beside, own, masked_t, total):
    blocks, _, edge = masked_t.shape
    for d in range(blocks):
        rows = pl.ds(d * edge, edge)
        kept = jnp.where(pre[rows, :].astype(jnp.float32) > 0, up[rows, :], 0.0)
        masked_t[d] = kept.T.astype(jnp.bfloat16)
    total[...] = jnp.zeros_like(total)
    live = count[0]

    def body(group, carry):
        for u in range(GROUP):
            slot = group * GROUP + u
            dst = slots[slot, 0] - base[0]
            src = slots[slot, 1] - base[1]
            tile = tiles[slots[slot, 2]]
            tile = jnp.where(slot < live, tile, jnp.zeros_like(tile))
            total[src] += jnp.dot(masked_t[dst], tile, preferred_element_type=jnp.float32)
        return carry

    lax.fori_loop(0, (live + GROUP - 1) // GROUP, body, 0)
    width = own.shape[0]
    beside[0] = total[pl.ds(0, width)].astype(jnp.bfloat16)
    own[...] = total[pl.ds(width, width)]
    beside[1] = total[pl.ds(2 * width, width)].astype(jnp.bfloat16)


def split(value):
    high = value.astype(jnp.bfloat16)
    return high, (value - high.astype(jnp.float32)).astype(jnp.bfloat16)


def weight_kernel(parts, features, summed, term):
    peers, blocks, _, edge = parts.shape
    acc = None
    for b in range(blocks):
        g = parts[0, b].astype(jnp.float32)
        for p in range(1, peers):
            g = g + parts[p, b].astype(jnp.float32)
        summed[b] = g
        feat = features[pl.ds(b * edge, edge), :]
        for piece in split(g):
            prod = jnp.dot(piece, feat, preferred_element_type=jnp.float32)
            acc = prod if acc is None else acc + prod
    term[...] = acc.T


def feature_kernel(summed, weight, grad):
    blocks, _, edge = summed.shape
    for b in range(blocks):
        acc = None
        for piece in split(summed[b].T):
            prod = lax.dot_general(
                piece, weight[...], (((1,), (1,)), ((), ())), preferred_element_type=jnp.float32
            )
            acc = prod if acc is None else acc + prod
        grad[pl.ds(b * edge, edge), :] = acc


def local(features, pre_act, upstream, weight, tile_values, tile_list, tile_counts, *, sizes):
    y, zc, x = sizes
    rows = y * zc
    own_row = lax.axis_index(("y", "zc"))
    own_col = lax.axis_index("x")
    rows_dev, channels = features.shape
    edge = tile_values.shape[1]
    blocks = rows_dev // edge
    width = x * blocks
    base = jnp.stack([(own_row * x + own_col) * blocks, (own_row - 1) * width]).astype(jnp.int32)
    params = pltpu.CompilerParams(vmem_limit_bytes=40 << 20)
    beside, own = pl.pallas_call(
        tile_kernel,
        out_shape=(
            jax.ShapeDtypeStruct((2, width, channels, edge), jnp.bfloat16),
            jax.ShapeDtypeStruct((width, channels, edge), jnp.float32),
        ),
        in_specs=[SMEM] * 3 + [VMEM] * 3,
        out_specs=(VMEM, VMEM),
        scratch_shapes=[
            pltpu.VMEM((blocks, channels, edge), jnp.bfloat16),
            pltpu.VMEM((3 * width, channels, edge), jnp.float32),
        ],
        compiler_params=params,
        name="tile_sums",
    )(base, tile_counts, tile_list, pre_act, upstream, tile_values)
    ring = ("y", "zc")
    from_next = lax.ppermute(beside[0], ring, [(i + 1, i) for i in range(rows - 1)])
    from_last = lax.ppermute(beside[1], ring, [(i, i + 1) for i in range(rows - 1)])
    summed = own + from_next.astype(jnp.float32) + from_last.astype(jnp.float32)
    summed = summed.astype(jnp.bfloat16).reshape(x, blocks, channels, edge)
    parts = lax.all_to_all(summed, "x", 0, 0)
    grad_t, term = pl.pallas_call(
        weight_kernel,
        out_shape=(
            jax.ShapeDtypeStruct((blocks, channels, edge), jnp.float32),
            jax.ShapeDtypeStruct((channels, channels), jnp.float32),
        ),
        in_specs=[VMEM] * 2,
        out_specs=(VMEM, VMEM),
        compiler_params=params,
        name="weight_term",
    )(parts, features)
    grad_features = pl.pallas_call(
        feature_kernel,
        out_shape=jax.ShapeDtypeStruct((rows_dev, channels), jnp.float32),
        in_specs=[VMEM] * 2,
        out_specs=VMEM,
        compiler_params=params,
        name="feature_grad",
    )(grad_t, weight)
    peers = y * x
    pieces = lax.all_to_all(term.reshape(peers, channels // peers, channels), ("y", "x"), 0, 0)
    piece = jnp.sum(pieces, axis=0)
    copies = jnp.broadcast_to(piece[None], (zc,) + piece.shape)
    piece = jnp.sum(lax.all_to_all(copies, "zc", 0, 0), axis=0)
    piece = piece / math.sqrt(rows * x * rows_dev)
    copies = jnp.broadcast_to(piece[None], (peers,) + piece.shape)
    grad_weight = lax.all_to_all(copies, ("y", "x"), 0, 0).reshape(channels, channels)
    return (grad_features, grad_weight)


def solution(mesh):
    rows, x = mesh.devices.shape
    y = math.gcd(rows, 8)
    zc = rows // y
    fine = Mesh(mesh.devices.reshape(y, zc, x), ("y", "zc", "x"))
    every = ("y", "zc", "x")
    return jax.shard_map(
        functools.partial(local, sizes=(y, zc, x)),
        mesh=fine,
        in_specs=(
            P(every, None),
            P(every, None),
            P(every, None),
            P(),
            P(every, None, None),
            P(every, None),
            P(every),
        ),
        out_specs=(P(every, None), P()),
        check_vma=False,
    )
```

```python
import functools
import math

import jax
import jax.numpy as jnp
from jax import lax
from jax.experimental import pallas as pl
from jax.experimental.pallas import tpu as pltpu
from jax.sharding import Mesh, PartitionSpec as P

GROUP = 24
VMEM = pl.BlockSpec(memory_space=pltpu.VMEM)
SMEM = pl.BlockSpec(memory_space=pltpu.SMEM)
HBM = pl.BlockSpec(memory_space=pltpu.HBM)


def tile_kernel(
    count, slots_hbm, pre_hbm, up_hbm, tiles_hbm,
    cross, chip, own,
    slots, pre, up, tiles, masked_t, total, arrived,
):
    pairs = ((slots_hbm, slots), (up_hbm, up), (pre_hbm, pre), (tiles_hbm, tiles))
    copies = [pltpu.make_async_copy(a, b, arrived.at[i]) for i, (a, b) in enumerate(pairs)]
    for copy in copies:
        copy.start()
    total[...] = jnp.zeros_like(total)
    blocks, _, edge = masked_t.shape
    width = own.shape[0]
    copies[1].wait()
    copies[2].wait()
    for d in range(blocks):
        rows = pl.ds(d * edge, edge)
        kept = jnp.where(pre[rows, :].astype(jnp.float32) > 0, up[rows, :], 0.0)
        masked_t[d] = kept.T.astype(jnp.bfloat16)
    copies[0].wait()
    copies[3].wait()
    live = count[0]
    row = slots[0, 0] // width
    first = (row - 1) * width

    def body(group, carry):
        for u in range(GROUP):
            slot = group * GROUP + u
            dst = slots[0, slot] % blocks
            src = slots[1, slot] - first
            tile = tiles[slots[2, slot]]
            tile = jnp.where(slot < live, tile, jnp.zeros_like(tile))
            total[src] += jnp.dot(masked_t[dst], tile, preferred_element_type=jnp.float32)
        return carry

    lax.fori_loop(0, (live + GROUP - 1) // GROUP, body, 0)
    core = row % 2
    cross[...] = total[pl.ds(2 * core * width, width)].astype(jnp.bfloat16)
    chip[...] = total[pl.ds(2 * (1 - core) * width, width)].astype(jnp.bfloat16)
    own[...] = total[pl.ds(width, width)]


def split(value):
    high = value.astype(jnp.bfloat16)
    return high, (value - high.astype(jnp.float32)).astype(jnp.bfloat16)


def weight_kernel(parts, features, summed, term):
    peers, blocks, _, edge = parts.shape
    acc = None
    for b in range(blocks):
        g = parts[0, b].astype(jnp.float32)
        for p in range(1, peers):
            g = g + parts[p, b].astype(jnp.float32)
        summed[b] = g
        feat = features[pl.ds(b * edge, edge), :]
        for piece in split(g):
            prod = jnp.dot(piece, feat, preferred_element_type=jnp.float32)
            acc = prod if acc is None else acc + prod
    acc = acc.T
    _, height, breadth = term.shape
    across = acc.shape[1] // breadth
    for i in range(acc.shape[0] // height):
        for j in range(across):
            term[i * across + j] = acc[
                i * height : (i + 1) * height, j * breadth : (j + 1) * breadth
            ]


def feature_kernel(summed, weight, grad):
    blocks, _, edge = summed.shape
    for b in range(blocks):
        acc = None
        for piece in split(summed[b].T):
            prod = lax.dot_general(
                piece, weight[...], (((1,), (1,)), ((), ())), preferred_element_type=jnp.float32
            )
            acc = prod if acc is None else acc + prod
        grad[pl.ds(b * edge, edge), :] = acc


def swap(array, axes, count, first):
    pairs = [(i, i + 1) for i in range(first, count - 1, 2)]
    return lax.ppermute(array, axes, pairs + [(j, i) for i, j in pairs])


def local(features, pre_act, upstream, weight, tile_values, tile_list, tile_counts, *, sizes):
    y, z, x = sizes
    rows = y * z * 2
    rows_dev, channels = features.shape
    slot_count, edge = tile_values.shape[:2]
    blocks = rows_dev // edge
    width = x * blocks
    params = pltpu.CompilerParams(vmem_limit_bytes=40 << 20)
    held = [
        pltpu.with_memory_space_constraint(a, pltpu.HBM)
        for a in (tile_list.T, pre_act, upstream, tile_values)
    ]
    cross, chip, own = pl.pallas_call(
        tile_kernel,
        out_shape=(
            jax.ShapeDtypeStruct((width, channels, edge), jnp.bfloat16),
            jax.ShapeDtypeStruct((width, channels, edge), jnp.bfloat16),
            jax.ShapeDtypeStruct((width, channels, edge), jnp.float32),
        ),
        in_specs=[SMEM] + [HBM] * 4,
        out_specs=(VMEM,) * 3,
        scratch_shapes=[
            pltpu.SMEM((3, slot_count), jnp.int32),
            pltpu.VMEM((rows_dev, channels), jnp.bfloat16),
            pltpu.VMEM((rows_dev, channels), jnp.float32),
            pltpu.VMEM((slot_count, edge, edge), jnp.bfloat16),
            pltpu.VMEM((blocks, channels, edge), jnp.bfloat16),
            pltpu.VMEM((3 * width, channels, edge), jnp.float32),
            pltpu.SemaphoreType.DMA((4,)),
        ],
        compiler_params=params,
        name="tile_sums",
    )(tile_counts, *held)
    from_cross = swap(cross, ("y", "z", "core"), rows, 1)
    from_chip = swap(chip, "core", 2, 0)
    summed = own + from_cross.astype(jnp.float32) + from_chip.astype(jnp.float32)
    summed = summed.astype(jnp.bfloat16).reshape(x, blocks, channels, edge)
    parts = lax.all_to_all(summed, "x", 0, 0)
    peers = y * 2 * x
    across = channels // 128
    height = channels * across // peers
    grad_t, term = pl.pallas_call(
        weight_kernel,
        out_shape=(
            jax.ShapeDtypeStruct((blocks, channels, edge), jnp.float32),
            jax.ShapeDtypeStruct((peers, height, 128), jnp.float32),
        ),
        in_specs=[VMEM] * 2,
        out_specs=(VMEM, VMEM),
        compiler_params=params,
        name="weight_term",
    )(parts, features)
    grad_features = pl.pallas_call(
        feature_kernel,
        out_shape=jax.ShapeDtypeStruct((rows_dev, channels), jnp.float32),
        in_specs=[VMEM] * 2,
        out_specs=VMEM,
        compiler_params=params,
        name="feature_grad",
    )(grad_t, weight)
    plane = ("y", "core", "x")
    piece = jnp.sum(lax.all_to_all(term, plane, 0, 0), axis=0)
    copies = jnp.broadcast_to(piece[None], (z,) + piece.shape)
    piece = jnp.sum(lax.all_to_all(copies, "z", 0, 0), axis=0)
    piece = piece / math.sqrt(rows * x * rows_dev)
    copies = jnp.broadcast_to(piece[None], (peers,) + piece.shape)
    pieces = lax.all_to_all(copies, plane, 0, 0).reshape(-1, across, height, 128)
    grad_weight = pieces.transpose(0, 2, 1, 3).reshape(channels, channels)
    return (grad_features, grad_weight)


def solution(mesh):
    rows, x = mesh.devices.shape
    y = math.gcd(rows, 8)
    z = rows // y // 2
    every = ("y", "z", "core", "x")
    fine = Mesh(mesh.devices.reshape(y, z, 2, x), every)
    return jax.shard_map(
        functools.partial(local, sizes=(y, z, x)),
        mesh=fine,
        in_specs=(
            P(every, None),
            P(every, None),
            P(every, None),
            P(),
            P(every, None, None),
            P(every, None),
            P(every),
        ),
        out_specs=(P(every, None), P()),
        check_vma=False,
    )
```

```python
import functools
import math

import jax
import jax.numpy as jnp
from jax import lax
from jax.experimental import pallas as pl
from jax.experimental.pallas import tpu as pltpu
from jax.sharding import Mesh, PartitionSpec as P

GROUP = 24
VMEM = pl.BlockSpec(memory_space=pltpu.VMEM)
SMEM = pl.BlockSpec(memory_space=pltpu.SMEM)
HBM = pl.BlockSpec(memory_space=pltpu.HBM)


def tile_kernel(
    count, slots_hbm, pre_hbm, up_hbm, tiles_hbm,
    cross, chip, own,
    slots, pre, up, tiles, masked_t, total, arrived,
):
    pairs = ((slots_hbm, slots), (up_hbm, up), (pre_hbm, pre), (tiles_hbm, tiles))
    copies = [pltpu.make_async_copy(a, b, arrived.at[i]) for i, (a, b) in enumerate(pairs)]
    for copy in copies:
        copy.start()
    total[...] = jnp.zeros_like(total)
    blocks, _, edge = masked_t.shape
    width = own.shape[0]
    copies[1].wait()
    copies[2].wait()
    for d in range(blocks):
        rows = pl.ds(d * edge, edge)
        kept = jnp.where(pre[rows, :].astype(jnp.float32) > 0, up[rows, :], 0.0)
        masked_t[d] = kept.T.astype(jnp.bfloat16)
    copies[0].wait()
    copies[3].wait()
    live = count[0]
    row = slots[0, 0] // width
    first = (row - 1) * width

    def body(group, carry):
        for u in range(GROUP):
            slot = group * GROUP + u
            dst = slots[0, slot] % blocks
            src = slots[1, slot] - first
            tile = tiles[slots[2, slot]]
            tile = jnp.where(slot < live, tile, jnp.zeros_like(tile))
            total[src] += jnp.dot(masked_t[dst], tile, preferred_element_type=jnp.float32)
        return carry

    lax.fori_loop(0, (live + GROUP - 1) // GROUP, body, 0)
    core = row % 2
    cross[...] = total[pl.ds(2 * core * width, width)].astype(jnp.bfloat16)
    chip[...] = total[pl.ds(2 * (1 - core) * width, width)].astype(jnp.bfloat16)
    own[...] = total[pl.ds(width, width)]


def split(value):
    high = value.astype(jnp.bfloat16)
    return high, (value - high.astype(jnp.float32)).astype(jnp.bfloat16)


def weight_kernel(own, cross, chip, features, packed):
    blocks, channels, edge = own.shape
    peers = packed.shape[0]
    each = blocks // peers
    acc = None
    for b in range(0, blocks, 2):
        pair = []
        for i in (b, b + 1):
            g = own[i] + cross[i].astype(jnp.float32) + chip[i].astype(jnp.float32)
            packed[i // each, pl.ds(i % each * channels, channels), :] = g.astype(jnp.bfloat16)
            pair.append(g)
        feat = features[pl.ds(b * edge, 2 * edge), :]
        for piece in split(jnp.concatenate(pair, axis=1)):
            prod = jnp.dot(piece, feat, preferred_element_type=jnp.float32)
            acc = prod if acc is None else acc + prod
    rows = acc.shape[1] // peers
    at = each * channels
    for piece in split(acc.T):
        for j in range(acc.shape[0] // edge):
            for c in range(peers):
                packed[c, pl.ds(at, rows), :] = piece[
                    c * rows : (c + 1) * rows, j * edge : (j + 1) * edge
                ]
            at += rows


def term_kernel(halves, packed, term):
    peers, depth, _ = packed.shape
    parts, both, _ = term.shape
    height = both // halves
    rows = parts * height
    start = depth - 2 * halves * rows
    for j in range(halves):
        acc = None
        for p in range(peers):
            for k in range(2):
                value = packed[p, pl.ds(start + (k * halves + j) * rows, rows), :]
                value = value.astype(jnp.float32)
                acc = value if acc is None else acc + value
        for q in range(parts):
            term[q, pl.ds(j * height, height), :] = acc[q * height : (q + 1) * height, :]


def spread_kernel(scale, got, copies):
    acc = got[0].astype(jnp.float32)
    for i in range(1, got.shape[0]):
        acc = acc + got[i].astype(jnp.float32)
    value = (acc / scale).astype(copies.dtype)
    for i in range(copies.shape[0]):
        copies[i] = value


def spread(got, count, scale):
    return pl.pallas_call(
        functools.partial(spread_kernel, scale),
        out_shape=jax.ShapeDtypeStruct((count,) + got.shape[1:], jnp.bfloat16),
        in_specs=[VMEM],
        out_specs=VMEM,
        compiler_params=pltpu.CompilerParams(vmem_limit_bytes=16 << 20),
        name="spread",
    )(got)


def feature_kernel(packed, weight, grad):
    peers, _, edge = packed.shape
    channels = weight.shape[0]
    for b in range(grad.shape[0] // edge):
        rows = pl.ds(b * channels, channels)
        g = packed[0, rows, :].astype(jnp.float32)
        for p in range(1, peers):
            g = g + packed[p, rows, :].astype(jnp.float32)
        acc = None
        for piece in split(g.T):
            prod = lax.dot_general(
                piece, weight[...], (((1,), (1,)), ((), ())), preferred_element_type=jnp.float32
            )
            acc = prod if acc is None else acc + prod
        grad[pl.ds(b * edge, edge), :] = acc


def swap(array, axes, count, first):
    pairs = [(i, i + 1) for i in range(first, count - 1, 2)]
    return lax.ppermute(array, axes, pairs + [(j, i) for i, j in pairs])


def local(features, pre_act, upstream, weight, tile_values, tile_list, tile_counts, *, sizes):
    y, z, x = sizes
    rows = y * z * 2
    rows_dev, channels = features.shape
    slot_count, edge = tile_values.shape[:2]
    blocks = rows_dev // edge
    width = x * blocks
    params = pltpu.CompilerParams(vmem_limit_bytes=40 << 20)
    group = lax.all_to_all(jnp.broadcast_to(features[None], (x,) + features.shape), "x", 0, 0)
    held = [
        pltpu.with_memory_space_constraint(a, pltpu.HBM)
        for a in (tile_list.T, pre_act, upstream, tile_values)
    ]
    cross, chip, own = pl.pallas_call(
        tile_kernel,
        out_shape=(
            jax.ShapeDtypeStruct((width, channels, edge), jnp.bfloat16),
            jax.ShapeDtypeStruct((width, channels, edge), jnp.bfloat16),
            jax.ShapeDtypeStruct((width, channels, edge), jnp.float32),
        ),
        in_specs=[SMEM] + [HBM] * 4,
        out_specs=(VMEM,) * 3,
        scratch_shapes=[
            pltpu.SMEM((3, slot_count), jnp.int32),
            pltpu.VMEM((rows_dev, channels), jnp.bfloat16),
            pltpu.VMEM((rows_dev, channels), jnp.float32),
            pltpu.VMEM((slot_count, edge, edge), jnp.bfloat16),
            pltpu.VMEM((blocks, channels, edge), jnp.bfloat16),
            pltpu.VMEM((3 * width, channels, edge), jnp.float32),
            pltpu.SemaphoreType.DMA((4,)),
        ],
        compiler_params=params,
        name="tile_sums",
    )(tile_counts, *held)
    from_cross = swap(cross, ("y", "z", "core"), rows, 1)
    from_chip = swap(chip, "core", 2, 0)
    halves = channels // edge
    height = channels // (x * y)
    packed = pl.pallas_call(
        weight_kernel,
        out_shape=jax.ShapeDtypeStruct(
            (x, blocks * channels + 2 * halves * channels // x, edge), jnp.bfloat16
        ),
        in_specs=[VMEM] * 4,
        out_specs=VMEM,
        compiler_params=params,
        name="weight_term",
    )(own, from_cross, from_chip, group.reshape(x * rows_dev, channels))
    packed = lax.all_to_all(packed, "x", 0, 0)
    term = pl.pallas_call(
        functools.partial(term_kernel, halves),
        out_shape=jax.ShapeDtypeStruct((y, halves * height, edge), jnp.float32),
        in_specs=[VMEM],
        out_specs=VMEM,
        compiler_params=params,
        name="term_sum",
    )(packed)
    grad_features = pl.pallas_call(
        feature_kernel,
        out_shape=jax.ShapeDtypeStruct((rows_dev, channels), jnp.float32),
        in_specs=[VMEM] * 2,
        out_specs=VMEM,
        compiler_params=params,
        name="feature_grad",
    )(packed, weight)
    got = lax.all_to_all(term, "y", 0, 0)
    copies = spread(got, 2 * z, math.sqrt(rows * x * rows_dev))
    got = lax.all_to_all(copies, ("z", "core"), 0, 0)
    copies = spread(got, x * y, 1.0)
    pieces = lax.all_to_all(copies, ("x", "y"), 0, 0).astype(jnp.float32)
    pieces = pieces.reshape(x * y, halves, height, edge)
    grad_weight = pieces.transpose(0, 2, 1, 3).reshape(channels, channels)
    return (grad_features, grad_weight)


def solution(mesh):
    rows, x = mesh.devices.shape
    y = math.gcd(rows, 8)
    z = rows // y // 2
    every = ("y", "z", "core", "x")
    fine = Mesh(mesh.devices.reshape(y, z, 2, x), every)
    return jax.shard_map(
        functools.partial(local, sizes=(y, z, x)),
        mesh=fine,
        in_specs=(
            P(every, None),
            P(every, None),
            P(every, None),
            P(),
            P(every, None, None),
            P(every, None),
            P(every),
        ),
        out_specs=(P(every, None), P()),
        check_vma=False,
    )
```

```python
import functools
import math

import jax
import jax.numpy as jnp
from jax import lax
from jax.experimental import pallas as pl
from jax.experimental.pallas import tpu as pltpu
from jax.sharding import Mesh, PartitionSpec as P

GROUP = 24
VMEM = pl.BlockSpec(memory_space=pltpu.VMEM)
SMEM = pl.BlockSpec(memory_space=pltpu.SMEM)
HBM = pl.BlockSpec(memory_space=pltpu.HBM)


def tile_kernel(
    count, slots_hbm, pre_hbm, up_hbm, tiles_hbm,
    cross, chip, own,
    slots, pre, up, tiles, masked_t, total, arrived,
):
    pairs = ((slots_hbm, slots), (up_hbm, up), (pre_hbm, pre), (tiles_hbm, tiles))
    copies = [pltpu.make_async_copy(a, b, arrived.at[i]) for i, (a, b) in enumerate(pairs)]
    for copy in copies:
        copy.start()
    total[...] = jnp.zeros_like(total)
    blocks, _, edge = masked_t.shape
    width = own.shape[0]
    copies[1].wait()
    copies[2].wait()
    for d in range(blocks):
        rows = pl.ds(d * edge, edge)
        kept = jnp.where(pre[rows, :].astype(jnp.float32) > 0, up[rows, :], 0.0)
        masked_t[d] = kept.T.astype(jnp.bfloat16)
    copies[0].wait()
    copies[3].wait()
    live = count[0]
    row = slots[0, 0] // width
    first = (row - 1) * width

    def body(group, carry):
        for u in range(GROUP):
            slot = group * GROUP + u
            dst = slots[0, slot] % blocks
            src = slots[1, slot] - first
            tile = tiles[slots[2, slot]]
            tile = jnp.where(slot < live, tile, jnp.zeros_like(tile))
            total[src] += jnp.dot(masked_t[dst], tile, preferred_element_type=jnp.float32)
        return carry

    lax.fori_loop(0, (live + GROUP - 1) // GROUP, body, 0)
    core = row % 2
    col = slots[0, 0] // blocks % (width // blocks)
    for k in range(width // blocks):
        to, at = pl.ds(k * blocks, blocks), (k ^ col) * blocks
        cross[to] = total[pl.ds(2 * core * width + at, blocks)].astype(jnp.bfloat16)
        chip[to] = total[pl.ds(2 * (1 - core) * width + at, blocks)].astype(jnp.bfloat16)
        own[to] = total[pl.ds(width + at, blocks)]


def split(value):
    high = value.astype(jnp.bfloat16)
    return high, (value - high.astype(jnp.float32)).astype(jnp.bfloat16)


def weight_kernel(own, cross, chip, feat0, feat1, feat32, give, keep0, keep3, term):
    blocks, channels, edge = keep0.shape
    held = []
    for k, (feat, at) in enumerate(((feat0, 0), (feat1, 0), (feat32, blocks), (feat32, 0))):
        for b in range(blocks):
            i = k * blocks + b
            g = own[i] + cross[i].astype(jnp.float32) + chip[i].astype(jnp.float32)
            if k == 0:
                keep0[b] = g
            elif k == 3:
                keep3[b] = g
            else:
                give[(k - 1) * blocks + b] = g.astype(jnp.bfloat16)
            held.append((g, feat, (at + b) * edge))
    acc = None
    for (g, feat, at), (g2, feat2, at2) in zip(held[::2], held[1::2]):
        rows = jnp.concatenate([feat[pl.ds(at, edge), :], feat2[pl.ds(at2, edge), :]], axis=0)
        for piece in split(jnp.concatenate([g, g2], axis=1)):
            prod = jnp.dot(piece, rows, preferred_element_type=jnp.float32)
            acc = prod if acc is None else acc + prod
    acc = acc.T
    parts, both, _ = term.shape
    height = acc.shape[0] // parts
    for i in range(parts):
        for j in range(both // height):
            term[i, pl.ds(j * height, height), :] = acc[
                i * height : (i + 1) * height, j * edge : (j + 1) * edge
            ]


def spread_kernel(scale, got, copies):
    acc = got[0].astype(jnp.float32)
    for i in range(1, got.shape[0]):
        acc = acc + got[i].astype(jnp.float32)
    value = (acc / scale).astype(copies.dtype)
    for i in range(copies.shape[0]):
        copies[i] = value


def spread(got, count, scale):
    return pl.pallas_call(
        functools.partial(spread_kernel, scale),
        out_shape=jax.ShapeDtypeStruct((count,) + got.shape[1:], jnp.bfloat16),
        in_specs=[VMEM],
        out_specs=VMEM,
        compiler_params=pltpu.CompilerParams(vmem_limit_bytes=16 << 20),
        name="spread",
    )(got)


def feature_kernel(keep, pair, other, weight, grad):
    blocks, _, edge = keep.shape
    for b in range(blocks):
        g = keep[b] + pair[b].astype(jnp.float32) + other[b].astype(jnp.float32)
        acc = None
        for piece in split(g.T):
            prod = lax.dot_general(
                piece, weight[...], (((1,), (1,)), ((), ())), preferred_element_type=jnp.float32
            )
            acc = prod if acc is None else acc + prod
        grad[pl.ds(b * edge, edge), :] = acc


def swap(array, axes, count, first):
    pairs = [(i, i + 1) for i in range(first, count - 1, 2)]
    return lax.ppermute(array, axes, pairs + [(j, i) for i, j in pairs])


def local(features, pre_act, upstream, weight, tile_values, tile_list, tile_counts, *, sizes):
    y, z, x = sizes
    rows = y * z * 2
    rows_dev, channels = features.shape
    slot_count, edge = tile_values.shape[:2]
    blocks = rows_dev // edge
    width = x * blocks
    params = pltpu.CompilerParams(vmem_limit_bytes=40 << 20)
    held = [
        pltpu.with_memory_space_constraint(a, pltpu.HBM)
        for a in (tile_list.T, pre_act, upstream, tile_values)
    ]
    cross, chip, own = pl.pallas_call(
        tile_kernel,
        out_shape=(
            jax.ShapeDtypeStruct((width, channels, edge), jnp.bfloat16),
            jax.ShapeDtypeStruct((width, channels, edge), jnp.bfloat16),
            jax.ShapeDtypeStruct((width, channels, edge), jnp.float32),
        ),
        in_specs=[SMEM] + [HBM] * 4,
        out_specs=(VMEM,) * 3,
        scratch_shapes=[
            pltpu.SMEM((3, slot_count), jnp.int32),
            pltpu.VMEM((rows_dev, channels), jnp.bfloat16),
            pltpu.VMEM((rows_dev, channels), jnp.float32),
            pltpu.VMEM((slot_count, edge, edge), jnp.bfloat16),
            pltpu.VMEM((blocks, channels, edge), jnp.bfloat16),
            pltpu.VMEM((3 * width, channels, edge), jnp.float32),
            pltpu.SemaphoreType.DMA((4,)),
        ],
        compiler_params=params,
        name="tile_sums",
    )(tile_counts, *held)
    from_cross = swap(cross, ("y", "z", "core"), rows, 1)
    from_chip = swap(chip, "core", 2, 0)
    near = [(i, i ^ 1) for i in range(x)]
    far = [(i, i ^ 3) for i in range(x)]
    feat1 = lax.ppermute(features, "x", near)
    feat32 = lax.ppermute(jnp.concatenate([features, feat1], axis=0), "x", far)
    halves = channels // edge
    height = channels // (x * y)
    third = (blocks, channels, edge)
    give, keep0, keep3, term = pl.pallas_call(
        weight_kernel,
        out_shape=(
            jax.ShapeDtypeStruct((2 * blocks, channels, edge), jnp.bfloat16),
            jax.ShapeDtypeStruct(third, jnp.float32),
            jax.ShapeDtypeStruct(third, jnp.float32),
            jax.ShapeDtypeStruct((x * y, halves * height, edge), jnp.float32),
        ),
        in_specs=[VMEM] * 6,
        out_specs=(VMEM,) * 4,
        compiler_params=params,
        name="weight_term",
    )(own, from_cross, from_chip, features, feat1, feat32)
    from_near = lax.ppermute(give, "x", near)
    onward = (keep3 + from_near[blocks:].astype(jnp.float32)).astype(jnp.bfloat16)
    from_far = lax.ppermute(onward, "x", far)
    grad_features = pl.pallas_call(
        feature_kernel,
        out_shape=jax.ShapeDtypeStruct((rows_dev, channels), jnp.float32),
        in_specs=[VMEM] * 4,
        out_specs=VMEM,
        compiler_params=params,
        name="feature_grad",
    )(keep0, from_near, from_far, weight)
    got = lax.all_to_all(term, ("x", "y"), 0, 0)
    copies = spread(got, 2 * z, math.sqrt(rows * x * rows_dev))
    got = lax.all_to_all(copies, ("z", "core"), 0, 0)
    copies = spread(got, x * y, 1.0)
    pieces = lax.all_to_all(copies, ("x", "y"), 0, 0).astype(jnp.float32)
    pieces = pieces.reshape(x * y, halves, height, edge)
    grad_weight = pieces.transpose(0, 2, 1, 3).reshape(channels, channels)
    return (grad_features, grad_weight)


def solution(mesh):
    rows, x = mesh.devices.shape
    y = math.gcd(rows, 8)
    z = rows // y // 2
    every = ("y", "z", "core", "x")
    fine = Mesh(mesh.devices.reshape(y, z, 2, x), every)
    return jax.shard_map(
        functools.partial(local, sizes=(y, z, x)),
        mesh=fine,
        in_specs=(
            P(every, None),
            P(every, None),
            P(every, None),
            P(),
            P(every, None, None),
            P(every, None),
            P(every),
        ),
        out_specs=(P(every, None), P()),
        check_vma=False,
    )
```

```python
import functools
import math

import jax
import jax.numpy as jnp
from jax import lax
from jax.experimental import pallas as pl
from jax.experimental.pallas import tpu as pltpu
from jax.sharding import Mesh, PartitionSpec as P

GROUP = 24
VMEM = pl.BlockSpec(memory_space=pltpu.VMEM)
SMEM = pl.BlockSpec(memory_space=pltpu.SMEM)
HBM = pl.BlockSpec(memory_space=pltpu.HBM)


def tile_kernel(
    count, slots_hbm, pre_hbm, up_hbm, tiles_hbm,
    cross, chip, own,
    slots, pre, up, tiles, masked_t, total, arrived,
):
    pairs = ((slots_hbm, slots), (up_hbm, up), (pre_hbm, pre), (tiles_hbm, tiles))
    copies = [pltpu.make_async_copy(a, b, arrived.at[i]) for i, (a, b) in enumerate(pairs)]
    for copy in copies:
        copy.start()
    total[...] = jnp.zeros_like(total)
    blocks, _, edge = masked_t.shape
    width = own.shape[0]
    copies[1].wait()
    copies[2].wait()
    for d in range(blocks):
        rows = pl.ds(d * edge, edge)
        kept = jnp.where(pre[rows, :].astype(jnp.float32) > 0, up[rows, :], 0.0)
        masked_t[d] = kept.T.astype(jnp.bfloat16)
    copies[0].wait()
    copies[3].wait()
    live = count[0]
    row = slots[0, 0] // width
    first = (row - 1) * width

    def body(group, carry):
        for u in range(GROUP):
            slot = group * GROUP + u
            dst = slots[0, slot] % blocks
            src = slots[1, slot] - first
            tile = tiles[slots[2, slot]]
            tile = jnp.where(slot < live, tile, jnp.zeros_like(tile))
            total[src] += jnp.dot(masked_t[dst], tile, preferred_element_type=jnp.float32)
        return carry

    lax.fori_loop(0, (live + GROUP - 1) // GROUP, body, 0)
    core = row % 2
    col = slots[0, 0] // blocks % (width // blocks)
    for k in range(width // blocks):
        to, at = pl.ds(k * blocks, blocks), (k ^ col) * blocks
        cross[to] = total[pl.ds(2 * core * width + at, blocks)].astype(jnp.bfloat16)
        chip[to] = total[pl.ds(2 * (1 - core) * width + at, blocks)].astype(jnp.bfloat16)
        own[to] = total[pl.ds(width + at, blocks)]


def split(value):
    high = value.astype(jnp.bfloat16)
    return high, (value - high.astype(jnp.float32)).astype(jnp.bfloat16)


def weight_kernel(own, cross, chip, feat0, feat1, feat32, give, keep0, keep3, term):
    blocks, channels, edge = keep0.shape
    held = []
    for k, (feat, at) in enumerate(((feat0, 0), (feat1, 0), (feat32, blocks), (feat32, 0))):
        for b in range(blocks):
            i = k * blocks + b
            g = own[i] + cross[i].astype(jnp.float32) + chip[i].astype(jnp.float32)
            if k == 0:
                keep0[b] = g
            elif k == 3:
                keep3[b] = g
            else:
                give[(k - 1) * blocks + b] = g.astype(jnp.bfloat16)
            held.append((g, feat, (at + b) * edge))
    acc = None
    for (g, feat, at), (g2, feat2, at2) in zip(held[::2], held[1::2]):
        rows = jnp.concatenate([feat[pl.ds(at, edge), :], feat2[pl.ds(at2, edge), :]], axis=0)
        for piece in split(jnp.concatenate([g, g2], axis=1)):
            prod = jnp.dot(piece, rows, preferred_element_type=jnp.float32)
            acc = prod if acc is None else acc + prod
    acc = acc.T
    parts, both, _ = term.shape
    height = acc.shape[0] // parts
    for i in range(parts):
        for j in range(both // height):
            term[i, pl.ds(j * height, height), :] = acc[
                i * height : (i + 1) * height, j * edge : (j + 1) * edge
            ]


def spread_kernel(scale, got, copies):
    acc = got[0].astype(jnp.float32)
    for i in range(1, got.shape[0]):
        acc = acc + got[i].astype(jnp.float32)
    value = (acc / scale).astype(copies.dtype)
    for i in range(copies.shape[0]):
        copies[i] = value


def spread(got, count, scale):
    return pl.pallas_call(
        functools.partial(spread_kernel, scale),
        out_shape=jax.ShapeDtypeStruct((count,) + got.shape[1:], jnp.bfloat16),
        in_specs=[VMEM],
        out_specs=VMEM,
        compiler_params=pltpu.CompilerParams(vmem_limit_bytes=16 << 20),
        name="spread",
    )(got)


def feature_kernel(keep, pair, other, weight, grad):
    blocks, _, edge = keep.shape
    for b in range(blocks):
        g = keep[b] + pair[b].astype(jnp.float32) + other[b].astype(jnp.float32)
        acc = None
        for piece in split(g.T):
            prod = lax.dot_general(
                piece, weight[...], (((1,), (1,)), ((), ())), preferred_element_type=jnp.float32
            )
            acc = prod if acc is None else acc + prod
        grad[pl.ds(b * edge, edge), :] = acc


def swap(array, axes, count, first):
    pairs = [(i, i + 1) for i in range(first, count - 1, 2)]
    return lax.ppermute(array, axes, pairs + [(j, i) for i, j in pairs])


def local(features, pre_act, upstream, weight, tile_values, tile_list, tile_counts, *, sizes):
    y, z, x = sizes
    rows = y * z * 2
    rows_dev, channels = features.shape
    slot_count, edge = tile_values.shape[:2]
    blocks = rows_dev // edge
    width = x * blocks
    params = pltpu.CompilerParams(vmem_limit_bytes=40 << 20)
    held = [
        pltpu.with_memory_space_constraint(a, pltpu.HBM)
        for a in (tile_list.T, pre_act, upstream, tile_values)
    ]
    cross, chip, own = pl.pallas_call(
        tile_kernel,
        out_shape=(
            jax.ShapeDtypeStruct((width, channels, edge), jnp.bfloat16),
            jax.ShapeDtypeStruct((width, channels, edge), jnp.bfloat16),
            jax.ShapeDtypeStruct((width, channels, edge), jnp.float32),
        ),
        in_specs=[SMEM] + [HBM] * 4,
        out_specs=(VMEM,) * 3,
        scratch_shapes=[
            pltpu.SMEM((3, slot_count), jnp.int32),
            pltpu.VMEM((rows_dev, channels), jnp.bfloat16),
            pltpu.VMEM((rows_dev, channels), jnp.float32),
            pltpu.VMEM((slot_count, edge, edge), jnp.bfloat16),
            pltpu.VMEM((blocks, channels, edge), jnp.bfloat16),
            pltpu.VMEM((3 * width, channels, edge), jnp.float32),
            pltpu.SemaphoreType.DMA((4,)),
        ],
        compiler_params=params,
        name="tile_sums",
    )(tile_counts, *held)
    near = [(i, i ^ 1) for i in range(x)]
    feat1 = lax.ppermute(features, "x", near)
    chip, feat1 = lax.optimization_barrier((chip, feat1))
    from_cross = swap(cross, ("y", "z", "core"), rows, 1)
    from_chip = swap(chip, "core", 2, 0)
    far = [(i, i ^ 3) for i in range(x)]
    feat32 = lax.ppermute(jnp.concatenate([features, feat1], axis=0), "x", far)
    halves = channels // edge
    height = channels // (x * y)
    third = (blocks, channels, edge)
    give, keep0, keep3, term = pl.pallas_call(
        weight_kernel,
        out_shape=(
            jax.ShapeDtypeStruct((2 * blocks, channels, edge), jnp.bfloat16),
            jax.ShapeDtypeStruct(third, jnp.float32),
            jax.ShapeDtypeStruct(third, jnp.float32),
            jax.ShapeDtypeStruct((x * y, halves * height, edge), jnp.float32),
        ),
        in_specs=[VMEM] * 6,
        out_specs=(VMEM,) * 4,
        compiler_params=params,
        name="weight_term",
    )(own, from_cross, from_chip, features, feat1, feat32)
    from_near = lax.ppermute(give, "x", near)
    onward = (keep3 + from_near[blocks:].astype(jnp.float32)).astype(jnp.bfloat16)
    from_far = lax.ppermute(onward, "x", far)
    grad_features = pl.pallas_call(
        feature_kernel,
        out_shape=jax.ShapeDtypeStruct((rows_dev, channels), jnp.float32),
        in_specs=[VMEM] * 4,
        out_specs=VMEM,
        compiler_params=params,
        name="feature_grad",
    )(keep0, from_near, from_far, weight)
    got = lax.all_to_all(term, ("x", "y"), 0, 0)
    copies = spread(got, 2 * z, math.sqrt(rows * x * rows_dev))
    got = lax.all_to_all(copies, ("z", "core"), 0, 0)
    got, from_far = lax.optimization_barrier((got, from_far))
    copies = spread(got, x * y, 1.0)
    pieces = lax.all_to_all(copies, ("x", "y"), 0, 0).astype(jnp.float32)
    pieces = pieces.reshape(x * y, halves, height, edge)
    grad_weight = pieces.transpose(0, 2, 1, 3).reshape(channels, channels)
    return (grad_features, grad_weight)


def solution(mesh):
    rows, x = mesh.devices.shape
    y = math.gcd(rows, 8)
    z = rows // y // 2
    every = ("y", "z", "core", "x")
    fine = Mesh(mesh.devices.reshape(y, z, 2, x), every)
    return jax.shard_map(
        functools.partial(local, sizes=(y, z, x)),
        mesh=fine,
        in_specs=(
            P(every, None),
            P(every, None),
            P(every, None),
            P(),
            P(every, None, None),
            P(every, None),
            P(every),
        ),
        out_specs=(P(every, None), P()),
        check_vma=False,
    )
```

```python
import functools
import math

import jax
import jax.numpy as jnp
from jax import lax
from jax.experimental import pallas as pl
from jax.experimental.pallas import tpu as pltpu
from jax.sharding import Mesh, PartitionSpec as P

GROUP = 24
VMEM = pl.BlockSpec(memory_space=pltpu.VMEM)
SMEM = pl.BlockSpec(memory_space=pltpu.SMEM)
HBM = pl.BlockSpec(memory_space=pltpu.HBM)


def tile_kernel(
    count, slots_hbm, pre_hbm, up_hbm, tiles_hbm,
    cross, chip, own,
    slots, pre, up, tiles, masked_t, total, arrived,
):
    pairs = ((slots_hbm, slots), (up_hbm, up), (pre_hbm, pre), (tiles_hbm, tiles))
    copies = [pltpu.make_async_copy(a, b, arrived.at[i]) for i, (a, b) in enumerate(pairs)]
    for copy in copies:
        copy.start()
    total[...] = jnp.zeros_like(total)
    blocks, _, edge = masked_t.shape
    width = own.shape[0]
    copies[1].wait()
    copies[2].wait()
    for d in range(blocks):
        rows = pl.ds(d * edge, edge)
        kept = jnp.where(pre[rows, :].astype(jnp.float32) > 0, up[rows, :], 0.0)
        masked_t[d] = kept.T.astype(jnp.bfloat16)
    copies[0].wait()
    copies[3].wait()
    live = count[0]
    row = slots[0, 0] // width
    first = (row - 1) * width

    def body(group, carry):
        for u in range(GROUP):
            slot = group * GROUP + u
            dst = slots[0, slot] % blocks
            src = slots[1, slot] - first
            tile = tiles[slots[2, slot]]
            tile = jnp.where(slot < live, tile, jnp.zeros_like(tile))
            total[src] += jnp.dot(masked_t[dst], tile, preferred_element_type=jnp.float32)
        return carry

    lax.fori_loop(0, (live + GROUP - 1) // GROUP, body, 0)
    core = row % 2
    cols = width // blocks
    col = slots[0, 0] // blocks % cols
    for k in range(cols):
        to = pl.ds(k * blocks, blocks)
        ahead, back = (k ^ col) * blocks, ((cols - k) % cols ^ col) * blocks
        mine, other = jnp.where(core == 0, ahead, back), jnp.where(core == 0, back, ahead)
        cross[to] = total[pl.ds(2 * core * width + other, blocks)].astype(jnp.bfloat16)
        chip[to] = total[pl.ds(2 * (1 - core) * width + other, blocks)].astype(jnp.bfloat16)
        own[to] = total[pl.ds(width + mine, blocks)]


def split(value):
    high = value.astype(jnp.bfloat16)
    return high, (value - high.astype(jnp.float32)).astype(jnp.bfloat16)


def weight_kernel(own, cross, chip, feat0, feat1, feat32, give, keep0, keep3, term):
    blocks, channels, edge = keep0.shape
    held = []
    for k, (feat, at) in enumerate(((feat0, 0), (feat1, 0), (feat32, blocks), (feat32, 0))):
        for b in range(blocks):
            i = k * blocks + b
            g = own[i] + cross[i].astype(jnp.float32) + chip[i].astype(jnp.float32)
            if k == 0:
                keep0[b] = g
            elif k == 3:
                keep3[b] = g
            else:
                give[(k - 1) * blocks + b] = g.astype(jnp.bfloat16)
            held.append((g, feat, (at + b) * edge))
    acc = None
    for (g, feat, at), (g2, feat2, at2) in zip(held[::2], held[1::2]):
        rows = jnp.concatenate([feat[pl.ds(at, edge), :], feat2[pl.ds(at2, edge), :]], axis=0)
        for piece in split(jnp.concatenate([g, g2], axis=1)):
            prod = jnp.dot(piece, rows, preferred_element_type=jnp.float32)
            acc = prod if acc is None else acc + prod
    acc = acc.T
    parts, both, _ = term.shape
    height = acc.shape[0] // parts
    for i in range(parts):
        for j in range(both // height):
            term[i, pl.ds(j * height, height), :] = acc[
                i * height : (i + 1) * height, j * edge : (j + 1) * edge
            ]


def spread_kernel(scale, got, copies):
    acc = got[0].astype(jnp.float32)
    for i in range(1, got.shape[0]):
        acc = acc + got[i].astype(jnp.float32)
    value = (acc / scale).astype(copies.dtype)
    for i in range(copies.shape[0]):
        copies[i] = value


def spread(got, count, scale):
    return pl.pallas_call(
        functools.partial(spread_kernel, scale),
        out_shape=jax.ShapeDtypeStruct((count,) + got.shape[1:], jnp.bfloat16),
        in_specs=[VMEM],
        out_specs=VMEM,
        compiler_params=pltpu.CompilerParams(vmem_limit_bytes=16 << 20),
        name="spread",
    )(got)


def feature_kernel(keep, pair, other, weight, grad):
    blocks, _, edge = keep.shape
    for b in range(blocks):
        g = keep[b] + pair[b].astype(jnp.float32) + other[b].astype(jnp.float32)
        acc = None
        for piece in split(g.T):
            prod = lax.dot_general(
                piece, weight[...], (((1,), (1,)), ((), ())), preferred_element_type=jnp.float32
            )
            acc = prod if acc is None else acc + prod
        grad[pl.ds(b * edge, edge), :] = acc


def hops(cols, flips):
    return [(c * cols + i, c * cols + (i ^ flip)) for c, flip in enumerate(flips) for i in range(cols)]


def swap(array, axes, count, first):
    pairs = [(i, i + 1) for i in range(first, count - 1, 2)]
    return lax.ppermute(array, axes, pairs + [(j, i) for i, j in pairs])


def local(features, pre_act, upstream, weight, tile_values, tile_list, tile_counts, *, sizes):
    y, z, x = sizes
    rows = y * z * 2
    rows_dev, channels = features.shape
    slot_count, edge = tile_values.shape[:2]
    blocks = rows_dev // edge
    width = x * blocks
    params = pltpu.CompilerParams(vmem_limit_bytes=40 << 20)
    held = [
        pltpu.with_memory_space_constraint(a, pltpu.HBM)
        for a in (tile_list.T, pre_act, upstream, tile_values)
    ]
    cross, chip, own = pl.pallas_call(
        tile_kernel,
        out_shape=(
            jax.ShapeDtypeStruct((width, channels, edge), jnp.bfloat16),
            jax.ShapeDtypeStruct((width, channels, edge), jnp.bfloat16),
            jax.ShapeDtypeStruct((width, channels, edge), jnp.float32),
        ),
        in_specs=[SMEM] + [HBM] * 4,
        out_specs=(VMEM,) * 3,
        scratch_shapes=[
            pltpu.SMEM((3, slot_count), jnp.int32),
            pltpu.VMEM((rows_dev, channels), jnp.bfloat16),
            pltpu.VMEM((rows_dev, channels), jnp.float32),
            pltpu.VMEM((slot_count, edge, edge), jnp.bfloat16),
            pltpu.VMEM((blocks, channels, edge), jnp.bfloat16),
            pltpu.VMEM((3 * width, channels, edge), jnp.float32),
            pltpu.SemaphoreType.DMA((4,)),
        ],
        compiler_params=params,
        name="tile_sums",
    )(tile_counts, *held)
    near, far = hops(x, (1, 3)), hops(x, (3, 1))
    feat1 = lax.ppermute(features, ("core", "x"), near)
    chip, feat1 = lax.optimization_barrier((chip, feat1))
    from_cross = swap(cross, ("y", "z", "core"), rows, 1)
    from_chip = swap(chip, "core", 2, 0)
    feat32 = lax.ppermute(jnp.concatenate([features, feat1], axis=0), ("core", "x"), far)
    halves = channels // edge
    height = channels // (x * y)
    third = (blocks, channels, edge)
    give, keep0, keep3, term = pl.pallas_call(
        weight_kernel,
        out_shape=(
            jax.ShapeDtypeStruct((2 * blocks, channels, edge), jnp.bfloat16),
            jax.ShapeDtypeStruct(third, jnp.float32),
            jax.ShapeDtypeStruct(third, jnp.float32),
            jax.ShapeDtypeStruct((x * y, halves * height, edge), jnp.float32),
        ),
        in_specs=[VMEM] * 6,
        out_specs=(VMEM,) * 4,
        compiler_params=params,
        name="weight_term",
    )(own, from_cross, from_chip, features, feat1, feat32)
    from_near = lax.ppermute(give, ("core", "x"), near)
    onward = (keep3 + from_near[blocks:].astype(jnp.float32)).astype(jnp.bfloat16)
    from_far = lax.ppermute(onward, ("core", "x"), far)
    grad_features = pl.pallas_call(
        feature_kernel,
        out_shape=jax.ShapeDtypeStruct((rows_dev, channels), jnp.float32),
        in_specs=[VMEM] * 4,
        out_specs=VMEM,
        compiler_params=params,
        name="feature_grad",
    )(keep0, from_near, from_far, weight)
    got = lax.all_to_all(term, ("x", "y"), 0, 0)
    copies = spread(got, 2 * z, math.sqrt(rows * x * rows_dev))
    got = lax.all_to_all(copies, ("z", "core"), 0, 0)
    got, from_far = lax.optimization_barrier((got, from_far))
    copies = spread(got, x * y, 1.0)
    pieces = lax.all_to_all(copies, ("x", "y"), 0, 0).astype(jnp.float32)
    pieces = pieces.reshape(x * y, halves, height, edge)
    grad_weight = pieces.transpose(0, 2, 1, 3).reshape(channels, channels)
    return (grad_features, grad_weight)


def solution(mesh):
    rows, x = mesh.devices.shape
    y = math.gcd(rows, 8)
    z = rows // y // 2
    every = ("y", "z", "core", "x")
    fine = Mesh(mesh.devices.reshape(y, z, 2, x), every)
    return jax.shard_map(
        functools.partial(local, sizes=(y, z, x)),
        mesh=fine,
        in_specs=(
            P(every, None),
            P(every, None),
            P(every, None),
            P(),
            P(every, None, None),
            P(every, None),
            P(every),
        ),
        out_specs=(P(every, None), P()),
        check_vma=False,
    )
```

```python
import functools
import math

import jax
import jax.numpy as jnp
from jax import lax
from jax.experimental import pallas as pl
from jax.experimental.pallas import tpu as pltpu
from jax.sharding import Mesh, PartitionSpec as P

GROUP = 24
VMEM = pl.BlockSpec(memory_space=pltpu.VMEM)
SMEM = pl.BlockSpec(memory_space=pltpu.SMEM)
HBM = pl.BlockSpec(memory_space=pltpu.HBM)


def tile_kernel(
    count, slots_hbm, pre_hbm, up_hbm, tiles_hbm,
    cross, chip, own,
    slots, pre, up, tiles, masked_t, total, arrived,
):
    pairs = ((slots_hbm, slots), (up_hbm, up), (pre_hbm, pre), (tiles_hbm, tiles))
    copies = [pltpu.make_async_copy(a, b, arrived.at[i]) for i, (a, b) in enumerate(pairs)]
    for copy in copies:
        copy.start()
    total[...] = jnp.zeros_like(total)
    blocks, _, edge = masked_t.shape
    width = own.shape[0]
    copies[1].wait()
    copies[2].wait()
    for d in range(blocks):
        rows = pl.ds(d * edge, edge)
        kept = jnp.where(pre[rows, :].astype(jnp.float32) > 0, up[rows, :], 0.0)
        masked_t[d] = kept.T.astype(jnp.bfloat16)
    copies[0].wait()
    copies[3].wait()
    live = count[0]
    row = slots[0, 0] // width
    first = (row - 1) * width

    def body(group, carry):
        for u in range(GROUP):
            slot = group * GROUP + u
            dst = slots[0, slot] % blocks
            src = slots[1, slot] - first
            tile = tiles[slots[2, slot]]
            tile = jnp.where(slot < live, tile, jnp.zeros_like(tile))
            total[src] += jnp.dot(masked_t[dst], tile, preferred_element_type=jnp.float32)
        return carry

    lax.fori_loop(0, (live + GROUP - 1) // GROUP, body, 0)
    core = row % 2
    cols = width // blocks
    col = slots[0, 0] // blocks % cols
    for k in range(cols):
        to = pl.ds(k * blocks, blocks)
        ahead, back = (k ^ col) * blocks, ((cols - k) % cols ^ col) * blocks
        mine, other = jnp.where(core == 0, ahead, back), jnp.where(core == 0, back, ahead)
        cross[to] = total[pl.ds(2 * core * width + other, blocks)].astype(jnp.bfloat16)
        chip[to] = total[pl.ds(2 * (1 - core) * width + other, blocks)].astype(jnp.bfloat16)
        own[to] = total[pl.ds(width + mine, blocks)]


def split(value):
    high = value.astype(jnp.bfloat16)
    return high, (value - high.astype(jnp.float32)).astype(jnp.bfloat16)


def weight_kernel(own, cross, chip, feat0, feat1, feat32, give, keep0, keep3, term):
    blocks, channels, edge = keep0.shape
    held = []
    for k, (feat, at) in enumerate(((feat0, 0), (feat1, 0), (feat32, blocks), (feat32, 0))):
        for b in range(blocks):
            i = k * blocks + b
            g = own[i] + cross[i].astype(jnp.float32) + chip[i].astype(jnp.float32)
            if k == 0:
                keep0[b] = g
            elif k == 3:
                keep3[b] = g
            else:
                give[(k - 1) * blocks + b] = g.astype(jnp.bfloat16)
            held.append((g, feat, (at + b) * edge))
    acc = None
    for (g, feat, at), (g2, feat2, at2) in zip(held[::2], held[1::2]):
        rows = jnp.concatenate([feat[pl.ds(at, edge), :], feat2[pl.ds(at2, edge), :]], axis=0)
        for piece in split(jnp.concatenate([g, g2], axis=1)):
            prod = jnp.dot(piece, rows, preferred_element_type=jnp.float32)
            acc = prod if acc is None else acc + prod
    acc = acc.T
    parts, both, _ = term.shape
    height = acc.shape[0] // parts
    for i in range(parts):
        halves = [
            acc[i * height : (i + 1) * height, j * edge : (j + 1) * edge]
            for j in range(both // height)
        ]
        term[i] = jnp.concatenate(halves, axis=0).astype(term.dtype)


def spread_kernel(scale, got, copies):
    acc = got[0].astype(jnp.float32)
    for i in range(1, got.shape[0]):
        acc = acc + got[i].astype(jnp.float32)
    value = (acc / scale).astype(copies.dtype)
    for i in range(copies.shape[0]):
        copies[i] = value


def spread(got, count, scale):
    return pl.pallas_call(
        functools.partial(spread_kernel, scale),
        out_shape=jax.ShapeDtypeStruct((count,) + got.shape[1:], jnp.bfloat16),
        in_specs=[VMEM],
        out_specs=VMEM,
        compiler_params=pltpu.CompilerParams(vmem_limit_bytes=16 << 20),
        name="spread",
    )(got)


def feature_kernel(keep, pair, other, weight, grad):
    blocks, _, edge = keep.shape
    for b in range(blocks):
        g = keep[b] + pair[b].astype(jnp.float32) + other[b].astype(jnp.float32)
        acc = None
        for piece in split(g.T):
            prod = lax.dot_general(
                piece, weight[...], (((1,), (1,)), ((), ())), preferred_element_type=jnp.float32
            )
            acc = prod if acc is None else acc + prod
        grad[pl.ds(b * edge, edge), :] = acc


def hops(cols, flips):
    return [(c * cols + i, c * cols + (i ^ flip)) for c, flip in enumerate(flips) for i in range(cols)]


def swap(array, axes, count, first):
    pairs = [(i, i + 1) for i in range(first, count - 1, 2)]
    return lax.ppermute(array, axes, pairs + [(j, i) for i, j in pairs])


def local(features, pre_act, upstream, weight, tile_values, tile_list, tile_counts, *, sizes):
    y, z, x = sizes
    rows = y * z * 2
    rows_dev, channels = features.shape
    slot_count, edge = tile_values.shape[:2]
    blocks = rows_dev // edge
    width = x * blocks
    params = pltpu.CompilerParams(vmem_limit_bytes=40 << 20)
    held = [
        pltpu.with_memory_space_constraint(a, pltpu.HBM)
        for a in (tile_list.T, pre_act, upstream, tile_values)
    ]
    cross, chip, own = pl.pallas_call(
        tile_kernel,
        out_shape=(
            jax.ShapeDtypeStruct((width, channels, edge), jnp.bfloat16),
            jax.ShapeDtypeStruct((width, channels, edge), jnp.bfloat16),
            jax.ShapeDtypeStruct((width, channels, edge), jnp.float32),
        ),
        in_specs=[SMEM] + [HBM] * 4,
        out_specs=(VMEM,) * 3,
        scratch_shapes=[
            pltpu.SMEM((3, slot_count), jnp.int32),
            pltpu.VMEM((rows_dev, channels), jnp.bfloat16),
            pltpu.VMEM((rows_dev, channels), jnp.float32),
            pltpu.VMEM((slot_count, edge, edge), jnp.bfloat16),
            pltpu.VMEM((blocks, channels, edge), jnp.bfloat16),
            pltpu.VMEM((3 * width, channels, edge), jnp.float32),
            pltpu.SemaphoreType.DMA((4,)),
        ],
        compiler_params=params,
        name="tile_sums",
    )(tile_counts, *held)
    near, far = hops(x, (1, 3)), hops(x, (3, 1))
    feat1 = lax.ppermute(features, ("core", "x"), near)
    chip, feat1 = lax.optimization_barrier((chip, feat1))
    from_cross = swap(cross, ("y", "z", "core"), rows, 1)
    from_chip = swap(chip, "core", 2, 0)
    feat32 = lax.ppermute(jnp.concatenate([features, feat1], axis=0), ("core", "x"), far)
    halves = channels // edge
    height = channels // (x * y)
    third = (blocks, channels, edge)
    give, keep0, keep3, term = pl.pallas_call(
        weight_kernel,
        out_shape=(
            jax.ShapeDtypeStruct((2 * blocks, channels, edge), jnp.bfloat16),
            jax.ShapeDtypeStruct(third, jnp.float32),
            jax.ShapeDtypeStruct(third, jnp.float32),
            jax.ShapeDtypeStruct((x * y, halves * height, edge), jnp.bfloat16),
        ),
        in_specs=[VMEM] * 6,
        out_specs=(VMEM,) * 4,
        compiler_params=params,
        name="weight_term",
    )(own, from_cross, from_chip, features, feat1, feat32)
    from_near = lax.ppermute(give, ("core", "x"), near)
    onward = (keep3 + from_near[blocks:].astype(jnp.float32)).astype(jnp.bfloat16)
    from_far = lax.ppermute(onward, ("core", "x"), far)
    grad_features = pl.pallas_call(
        feature_kernel,
        out_shape=jax.ShapeDtypeStruct((rows_dev, channels), jnp.float32),
        in_specs=[VMEM] * 4,
        out_specs=VMEM,
        compiler_params=params,
        name="feature_grad",
    )(keep0, from_near, from_far, weight)
    got = lax.all_to_all(term, ("x", "y"), 0, 0)
    copies = spread(got, 2 * z, math.sqrt(rows * x * rows_dev))
    got = lax.all_to_all(copies, ("z", "core"), 0, 0)
    copies = spread(got, x * y, 1.0)
    pieces = lax.all_to_all(copies, ("x", "y"), 0, 0).astype(jnp.float32)
    pieces = pieces.reshape(x * y, halves, height, edge)
    grad_weight = pieces.transpose(0, 2, 1, 3).reshape(channels, channels)
    return (grad_features, grad_weight)


def solution(mesh):
    rows, x = mesh.devices.shape
    y = math.gcd(rows, 8)
    z = rows // y // 2
    every = ("y", "z", "core", "x")
    fine = Mesh(mesh.devices.reshape(y, z, 2, x), every)
    return jax.shard_map(
        functools.partial(local, sizes=(y, z, x)),
        mesh=fine,
        in_specs=(
            P(every, None),
            P(every, None),
            P(every, None),
            P(),
            P(every, None, None),
            P(every, None),
            P(every),
        ),
        out_specs=(P(every, None), P()),
        check_vma=False,
    )
```

```python
import functools
import math

import jax
import jax.numpy as jnp
from jax import lax
from jax.experimental import pallas as pl
from jax.experimental.pallas import tpu as pltpu
from jax.sharding import Mesh, PartitionSpec as P

GROUP = 24
VMEM = pl.BlockSpec(memory_space=pltpu.VMEM)
SMEM = pl.BlockSpec(memory_space=pltpu.SMEM)
HBM = pl.BlockSpec(memory_space=pltpu.HBM)


def tile_kernel(
    count, slots_hbm, pre_hbm, up_hbm, tiles_hbm,
    cross, chip, own,
    slots, pre, up, tiles, masked_t, total, arrived,
):
    pairs = ((slots_hbm, slots), (up_hbm, up), (pre_hbm, pre), (tiles_hbm, tiles))
    copies = [pltpu.make_async_copy(a, b, arrived.at[i]) for i, (a, b) in enumerate(pairs)]
    for copy in copies:
        copy.start()
    total[...] = jnp.zeros_like(total)
    blocks, _, edge = masked_t.shape
    width = own.shape[0]
    copies[1].wait()
    copies[2].wait()
    for d in range(blocks):
        rows = pl.ds(d * edge, edge)
        kept = jnp.where(pre[rows, :].astype(jnp.float32) > 0, up[rows, :], 0.0)
        masked_t[d] = kept.T.astype(jnp.bfloat16)
    copies[0].wait()
    copies[3].wait()
    live = count[0]
    row = slots[0, 0] // width
    first = (row - 1) * width

    def body(group, carry):
        for u in range(GROUP):
            slot = group * GROUP + u
            dst = slots[0, slot] % blocks
            src = slots[1, slot] - first
            tile = tiles[slots[2, slot]]
            tile = jnp.where(slot < live, tile, jnp.zeros_like(tile))
            total[src] += jnp.dot(masked_t[dst], tile, preferred_element_type=jnp.float32)
        return carry

    lax.fori_loop(0, (live + GROUP - 1) // GROUP, body, 0)
    core = row % 2
    cols = width // blocks
    col = slots[0, 0] // blocks % cols
    for k in range(cols):
        to = pl.ds(k * blocks, blocks)
        ahead, back = (k ^ col) * blocks, ((cols - k) % cols ^ col) * blocks
        mine, other = jnp.where(core == 0, ahead, back), jnp.where(core == 0, back, ahead)
        cross[to] = total[pl.ds(2 * core * width + other, blocks)].astype(jnp.bfloat16)
        chip[to] = total[pl.ds(2 * (1 - core) * width + other, blocks)].astype(jnp.bfloat16)
        own[to] = total[pl.ds(width + mine, blocks)]


def split(value):
    high = value.astype(jnp.bfloat16)
    return high, (value - high.astype(jnp.float32)).astype(jnp.bfloat16)


def weight_kernel(own, cross, chip, feat0, feat1, feat2, feat3, give1, give2, keep0, keep3, term):
    blocks, channels, edge = keep0.shape
    held = []
    for k, feat in enumerate((feat0, feat1, feat2, feat3)):
        for b in range(blocks):
            i = k * blocks + b
            g = own[i] + cross[i].astype(jnp.float32) + chip[i].astype(jnp.float32)
            if k == 0:
                keep0[b] = g
            elif k == 3:
                keep3[b] = g
            else:
                (give1 if k == 1 else give2)[b] = g.astype(jnp.bfloat16)
            held.append((g, feat, b * edge))
    acc = None
    for (g, feat, at), (g2, feat2, at2) in zip(held[::2], held[1::2]):
        rows = jnp.concatenate([feat[pl.ds(at, edge), :], feat2[pl.ds(at2, edge), :]], axis=0)
        for piece in split(jnp.concatenate([g, g2], axis=1)):
            prod = jnp.dot(piece, rows, preferred_element_type=jnp.float32)
            acc = prod if acc is None else acc + prod
    acc = acc.T
    parts, both, _ = term.shape
    height = acc.shape[0] // parts
    for i in range(parts):
        halves = [
            acc[i * height : (i + 1) * height, j * edge : (j + 1) * edge]
            for j in range(both // height)
        ]
        term[i] = jnp.concatenate(halves, axis=0).astype(term.dtype)


def spread_kernel(scale, got, copies):
    acc = got[0].astype(jnp.float32)
    for i in range(1, got.shape[0]):
        acc = acc + got[i].astype(jnp.float32)
    value = (acc / scale).astype(copies.dtype)
    for i in range(copies.shape[0]):
        copies[i] = value


def spread(got, count, scale):
    return pl.pallas_call(
        functools.partial(spread_kernel, scale),
        out_shape=jax.ShapeDtypeStruct((count,) + got.shape[1:], jnp.bfloat16),
        in_specs=[VMEM],
        out_specs=VMEM,
        compiler_params=pltpu.CompilerParams(vmem_limit_bytes=16 << 20),
        name="spread",
    )(got)


def feature_kernel(keep, pair, other, weight, grad):
    blocks, _, edge = keep.shape
    for b in range(blocks):
        g = keep[b] + pair[b].astype(jnp.float32) + other[b].astype(jnp.float32)
        acc = None
        for piece in split(g.T):
            prod = lax.dot_general(
                piece, weight[...], (((1,), (1,)), ((), ())), preferred_element_type=jnp.float32
            )
            acc = prod if acc is None else acc + prod
        grad[pl.ds(b * edge, edge), :] = acc


def hops(cols, flips):
    return [(c * cols + i, c * cols + (i ^ flip)) for c, flip in enumerate(flips) for i in range(cols)]


def swap(array, axes, count, first):
    pairs = [(i, i + 1) for i in range(first, count - 1, 2)]
    return lax.ppermute(array, axes, pairs + [(j, i) for i, j in pairs])


def local(features, pre_act, upstream, weight, tile_values, tile_list, tile_counts, *, sizes):
    y, z, x = sizes
    rows = y * z * 2
    rows_dev, channels = features.shape
    slot_count, edge = tile_values.shape[:2]
    blocks = rows_dev // edge
    width = x * blocks
    params = pltpu.CompilerParams(vmem_limit_bytes=40 << 20)
    held = [
        pltpu.with_memory_space_constraint(a, pltpu.HBM)
        for a in (tile_list.T, pre_act, upstream, tile_values)
    ]
    cross, chip, own = pl.pallas_call(
        tile_kernel,
        out_shape=(
            jax.ShapeDtypeStruct((width, channels, edge), jnp.bfloat16),
            jax.ShapeDtypeStruct((width, channels, edge), jnp.bfloat16),
            jax.ShapeDtypeStruct((width, channels, edge), jnp.float32),
        ),
        in_specs=[SMEM] + [HBM] * 4,
        out_specs=(VMEM,) * 3,
        scratch_shapes=[
            pltpu.SMEM((3, slot_count), jnp.int32),
            pltpu.VMEM((rows_dev, channels), jnp.bfloat16),
            pltpu.VMEM((rows_dev, channels), jnp.float32),
            pltpu.VMEM((slot_count, edge, edge), jnp.bfloat16),
            pltpu.VMEM((blocks, channels, edge), jnp.bfloat16),
            pltpu.VMEM((3 * width, channels, edge), jnp.float32),
            pltpu.SemaphoreType.DMA((4,)),
        ],
        compiler_params=params,
        name="tile_sums",
    )(tile_counts, *held)
    near, far = hops(x, (1, 3)), hops(x, (3, 1))
    feat1 = lax.ppermute(features, ("core", "x"), near)
    chip, feat1 = lax.optimization_barrier((chip, feat1))
    from_cross = swap(cross, ("y", "z", "core"), rows, 1)
    from_chip = swap(chip, "core", 2, 0)
    feat3 = lax.ppermute(features, ("core", "x"), far)
    feat2 = lax.ppermute(feat1, ("core", "x"), far)
    halves = channels // edge
    height = channels // (x * y)
    third = (blocks, channels, edge)
    give1, give2, keep0, keep3, term = pl.pallas_call(
        weight_kernel,
        out_shape=(
            jax.ShapeDtypeStruct(third, jnp.bfloat16),
            jax.ShapeDtypeStruct(third, jnp.bfloat16),
            jax.ShapeDtypeStruct(third, jnp.float32),
            jax.ShapeDtypeStruct(third, jnp.float32),
            jax.ShapeDtypeStruct((x * y, halves * height, edge), jnp.bfloat16),
        ),
        in_specs=[VMEM] * 7,
        out_specs=(VMEM,) * 5,
        compiler_params=params,
        name="weight_term",
    )(own, from_cross, from_chip, features, feat1, feat2, feat3)
    passing = lax.ppermute(give2, ("core", "x"), near)
    onward = (keep3 + passing.astype(jnp.float32)).astype(jnp.bfloat16)
    from_far = lax.ppermute(onward, ("core", "x"), far)
    got = lax.all_to_all(term, ("x", "y"), 0, 0)
    got, give1 = lax.optimization_barrier((got, give1))
    from_near = lax.ppermute(give1, ("core", "x"), near)
    copies = spread(got, 2 * z, math.sqrt(rows * x * rows_dev))
    got = lax.all_to_all(copies, ("z", "core"), 0, 0)
    got, from_near, from_far = lax.optimization_barrier((got, from_near, from_far))
    grad_features = pl.pallas_call(
        feature_kernel,
        out_shape=jax.ShapeDtypeStruct((rows_dev, channels), jnp.float32),
        in_specs=[VMEM] * 4,
        out_specs=VMEM,
        compiler_params=params,
        name="feature_grad",
    )(keep0, from_near, from_far, weight)
    copies = spread(got, x * y, 1.0)
    pieces = lax.all_to_all(copies, ("x", "y"), 0, 0).astype(jnp.float32)
    pieces = pieces.reshape(x * y, halves, height, edge)
    grad_weight = pieces.transpose(0, 2, 1, 3).reshape(channels, channels)
    return (grad_features, grad_weight)


def solution(mesh):
    rows, x = mesh.devices.shape
    y = math.gcd(rows, 8)
    z = rows // y // 2
    every = ("y", "z", "core", "x")
    fine = Mesh(mesh.devices.reshape(y, z, 2, x), every)
    return jax.shard_map(
        functools.partial(local, sizes=(y, z, x)),
        mesh=fine,
        in_specs=(
            P(every, None),
            P(every, None),
            P(every, None),
            P(),
            P(every, None, None),
            P(every, None),
            P(every),
        ),
        out_specs=(P(every, None), P()),
        check_vma=False,
    )
```

```python
import functools
import math

import jax
import jax.numpy as jnp
from jax import lax
from jax.experimental import pallas as pl
from jax.experimental.pallas import tpu as pltpu
from jax.sharding import Mesh, PartitionSpec as P

GROUP = 24
VMEM = pl.BlockSpec(memory_space=pltpu.VMEM)
SMEM = pl.BlockSpec(memory_space=pltpu.SMEM)
HBM = pl.BlockSpec(memory_space=pltpu.HBM)


def tile_kernel(
    count, slots_hbm, pre_hbm, up_hbm, tiles_hbm,
    cross, chip, own,
    slots, pre, up, tiles, masked_t, total, arrived,
):
    pairs = ((slots_hbm, slots), (up_hbm, up), (pre_hbm, pre), (tiles_hbm, tiles))
    copies = [pltpu.make_async_copy(a, b, arrived.at[i]) for i, (a, b) in enumerate(pairs)]
    for copy in copies:
        copy.start()
    total[...] = jnp.zeros_like(total)
    blocks, _, edge = masked_t.shape
    width = own.shape[0]
    copies[1].wait()
    copies[2].wait()
    for d in range(blocks):
        rows = pl.ds(d * edge, edge)
        kept = jnp.where(pre[rows, :].astype(jnp.float32) > 0, up[rows, :], 0.0)
        masked_t[d] = kept.T.astype(jnp.bfloat16)
    copies[0].wait()
    copies[3].wait()
    live = count[0]
    row = slots[0, 0] // width
    first = (row - 1) * width

    def body(group, carry):
        for u in range(GROUP):
            slot = group * GROUP + u
            dst = slots[0, slot] % blocks
            src = slots[1, slot] - first
            tile = tiles[slots[2, slot]]
            tile = jnp.where(slot < live, tile, jnp.zeros_like(tile))
            total[src] += jnp.dot(masked_t[dst], tile, preferred_element_type=jnp.float32)
        return carry

    lax.fori_loop(0, (live + GROUP - 1) // GROUP, body, 0)
    core = row % 2
    cols = width // blocks
    col = slots[0, 0] // blocks % cols
    for k in range(cols):
        to = pl.ds(k * blocks, blocks)
        ahead, back = (k ^ col) * blocks, ((cols - k) % cols ^ col) * blocks
        mine, other = jnp.where(core == 0, ahead, back), jnp.where(core == 0, back, ahead)
        cross[to] = total[pl.ds(2 * core * width + other, blocks)].astype(jnp.bfloat16)
        chip[to] = total[pl.ds(2 * (1 - core) * width + other, blocks)].astype(jnp.bfloat16)
        own[to] = total[pl.ds(width + mine, blocks)]


def split(value):
    high = value.astype(jnp.bfloat16)
    return high, (value - high.astype(jnp.float32)).astype(jnp.bfloat16)


def weight_kernel(own, cross, chip, feat0, feat1, feat2, feat3, give, keep0, keep3, term):
    blocks, channels, edge = keep0.shape
    held = []
    for k, feat in enumerate((feat0, feat1, feat2, feat3)):
        for b in range(blocks):
            i = k * blocks + b
            g = own[i] + cross[i].astype(jnp.float32) + chip[i].astype(jnp.float32)
            if k == 0:
                keep0[b] = g
            elif k == 3:
                keep3[b] = g
            else:
                give[(k - 1) * blocks + b] = g.astype(jnp.bfloat16)
            held.append((g, feat, b * edge))
    acc = None
    for (g, feat, at), (g2, feat2, at2) in zip(held[::2], held[1::2]):
        rows = jnp.concatenate([feat[pl.ds(at, edge), :], feat2[pl.ds(at2, edge), :]], axis=0)
        for piece in split(jnp.concatenate([g, g2], axis=1)):
            prod = jnp.dot(piece, rows, preferred_element_type=jnp.float32)
            acc = prod if acc is None else acc + prod
    acc = acc.T
    parts, both, _ = term.shape
    height = acc.shape[0] // parts
    for i in range(parts):
        halves = [
            acc[i * height : (i + 1) * height, j * edge : (j + 1) * edge]
            for j in range(both // height)
        ]
        term[i] = jnp.concatenate(halves, axis=0).astype(term.dtype)


def spread_kernel(scale, got, copies):
    acc = got[0].astype(jnp.float32)
    for i in range(1, got.shape[0]):
        acc = acc + got[i].astype(jnp.float32)
    value = (acc / scale).astype(copies.dtype)
    for i in range(copies.shape[0]):
        copies[i] = value


def spread(got, count, scale):
    return pl.pallas_call(
        functools.partial(spread_kernel, scale),
        out_shape=jax.ShapeDtypeStruct((count,) + got.shape[1:], jnp.bfloat16),
        in_specs=[VMEM],
        out_specs=VMEM,
        compiler_params=pltpu.CompilerParams(vmem_limit_bytes=16 << 20),
        name="spread",
    )(got)


def feature_kernel(keep, pair, other, weight, grad):
    blocks, _, edge = keep.shape
    for b in range(blocks):
        g = keep[b] + pair[b].astype(jnp.float32) + other[b].astype(jnp.float32)
        acc = None
        for piece in split(g.T):
            prod = lax.dot_general(
                piece, weight[...], (((1,), (1,)), ((), ())), preferred_element_type=jnp.float32
            )
            acc = prod if acc is None else acc + prod
        grad[pl.ds(b * edge, edge), :] = acc


def hops(cols, flips):
    return [(c * cols + i, c * cols + (i ^ flip)) for c, flip in enumerate(flips) for i in range(cols)]


def swap(array, axes, count, first):
    pairs = [(i, i + 1) for i in range(first, count - 1, 2)]
    return lax.ppermute(array, axes, pairs + [(j, i) for i, j in pairs])


def local(features, pre_act, upstream, weight, tile_values, tile_list, tile_counts, *, sizes):
    y, z, x = sizes
    rows = y * z * 2
    rows_dev, channels = features.shape
    slot_count, edge = tile_values.shape[:2]
    blocks = rows_dev // edge
    width = x * blocks
    params = pltpu.CompilerParams(vmem_limit_bytes=40 << 20)
    held = [
        pltpu.with_memory_space_constraint(a, pltpu.HBM)
        for a in (tile_list.T, pre_act, upstream, tile_values)
    ]
    cross, chip, own = pl.pallas_call(
        tile_kernel,
        out_shape=(
            jax.ShapeDtypeStruct((width, channels, edge), jnp.bfloat16),
            jax.ShapeDtypeStruct((width, channels, edge), jnp.bfloat16),
            jax.ShapeDtypeStruct((width, channels, edge), jnp.float32),
        ),
        in_specs=[SMEM] + [HBM] * 4,
        out_specs=(VMEM,) * 3,
        scratch_shapes=[
            pltpu.SMEM((3, slot_count), jnp.int32),
            pltpu.VMEM((rows_dev, channels), jnp.bfloat16),
            pltpu.VMEM((rows_dev, channels), jnp.float32),
            pltpu.VMEM((slot_count, edge, edge), jnp.bfloat16),
            pltpu.VMEM((blocks, channels, edge), jnp.bfloat16),
            pltpu.VMEM((3 * width, channels, edge), jnp.float32),
            pltpu.SemaphoreType.DMA((4,)),
        ],
        compiler_params=params,
        name="tile_sums",
    )(tile_counts, *held)
    near, far = hops(x, (1, 3)), hops(x, (3, 1))
    feat1 = lax.ppermute(features, ("core", "x"), near)
    from_cross = swap(cross, ("y", "z", "core"), rows, 1)
    from_chip = swap(chip, "core", 2, 0)
    feat3 = lax.ppermute(features, ("core", "x"), far)
    feat2 = lax.ppermute(feat1, ("core", "x"), far)
    halves = channels // edge
    height = channels // (x * y)
    third = (blocks, channels, edge)
    give, keep0, keep3, term = pl.pallas_call(
        weight_kernel,
        out_shape=(
            jax.ShapeDtypeStruct((2 * blocks, channels, edge), jnp.bfloat16),
            jax.ShapeDtypeStruct(third, jnp.float32),
            jax.ShapeDtypeStruct(third, jnp.float32),
            jax.ShapeDtypeStruct((x * y, halves * height, edge), jnp.bfloat16),
        ),
        in_specs=[VMEM] * 7,
        out_specs=(VMEM,) * 4,
        compiler_params=params,
        name="weight_term",
    )(own, from_cross, from_chip, features, feat1, feat2, feat3)
    from_near = lax.ppermute(give, ("core", "x"), near)
    onward = (keep3 + from_near[blocks:].astype(jnp.float32)).astype(jnp.bfloat16)
    from_far = lax.ppermute(onward, ("core", "x"), far)
    grad_features = pl.pallas_call(
        feature_kernel,
        out_shape=jax.ShapeDtypeStruct((rows_dev, channels), jnp.float32),
        in_specs=[VMEM] * 4,
        out_specs=VMEM,
        compiler_params=params,
        name="feature_grad",
    )(keep0, from_near, from_far, weight)
    got = lax.all_to_all(term, ("x", "y"), 0, 0)
    copies = spread(got, 2 * z, math.sqrt(rows * x * rows_dev))
    got = lax.all_to_all(copies, ("z", "core"), 0, 0)
    copies = spread(got, x * y, 1.0)
    pieces = lax.all_to_all(copies, ("x", "y"), 0, 0).astype(jnp.float32)
    pieces = pieces.reshape(x * y, halves, height, edge)
    grad_weight = pieces.transpose(0, 2, 1, 3).reshape(channels, channels)
    return (grad_features, grad_weight)


def solution(mesh):
    rows, x = mesh.devices.shape
    y = math.gcd(rows, 8)
    z = rows // y // 2
    every = ("y", "z", "core", "x")
    fine = Mesh(mesh.devices.reshape(y, z, 2, x), every)
    return jax.shard_map(
        functools.partial(local, sizes=(y, z, x)),
        mesh=fine,
        in_specs=(
            P(every, None),
            P(every, None),
            P(every, None),
            P(),
            P(every, None, None),
            P(every, None),
            P(every),
        ),
        out_specs=(P(every, None), P()),
        check_vma=False,
    )
```

```python
import functools
import math

import jax
import jax.numpy as jnp
from jax import lax
from jax.experimental import pallas as pl
from jax.experimental.pallas import tpu as pltpu
from jax.sharding import Mesh, PartitionSpec as P

GROUP = 24
VMEM = pl.BlockSpec(memory_space=pltpu.VMEM)
SMEM = pl.BlockSpec(memory_space=pltpu.SMEM)
HBM = pl.BlockSpec(memory_space=pltpu.HBM)


def tile_kernel(
    count, slots_hbm, pre_hbm, up_hbm, tiles_hbm,
    cross, chip, own,
    slots, pre, up, tiles, masked_t, total, arrived,
):
    pairs = ((slots_hbm, slots), (up_hbm, up), (pre_hbm, pre), (tiles_hbm, tiles))
    copies = [pltpu.make_async_copy(a, b, arrived.at[i]) for i, (a, b) in enumerate(pairs)]
    for copy in copies:
        copy.start()
    total[...] = jnp.zeros_like(total)
    blocks, _, edge = masked_t.shape
    width = own.shape[0]
    copies[1].wait()
    copies[2].wait()
    for d in range(blocks):
        rows = pl.ds(d * edge, edge)
        kept = jnp.where(pre[rows, :].astype(jnp.float32) > 0, up[rows, :], 0.0)
        masked_t[d] = kept.T.astype(jnp.bfloat16)
    copies[0].wait()
    copies[3].wait()
    live = count[0]
    row = slots[0, 0] // width
    first = (row - 1) * width

    def body(group, carry):
        for u in range(GROUP):
            slot = group * GROUP + u
            dst = slots[0, slot] % blocks
            src = slots[1, slot] - first
            tile = tiles[slots[2, slot]]
            tile = jnp.where(slot < live, tile, jnp.zeros_like(tile))
            total[src] += jnp.dot(masked_t[dst], tile, preferred_element_type=jnp.float32)
        return carry

    lax.fori_loop(0, (live + GROUP - 1) // GROUP, body, 0)
    core = row % 2
    cols = width // blocks
    col = slots[0, 0] // blocks % cols
    for k in range(cols):
        to = pl.ds(k * blocks, blocks)
        ahead, back = (k ^ col) * blocks, ((cols - k) % cols ^ col) * blocks
        mine, other = jnp.where(core == 0, ahead, back), jnp.where(core == 0, back, ahead)
        cross[to] = total[pl.ds(2 * core * width + other, blocks)].astype(jnp.bfloat16)
        chip[to] = total[pl.ds(2 * (1 - core) * width + other, blocks)].astype(jnp.bfloat16)
        own[to] = total[pl.ds(width + mine, blocks)]


def split(value):
    high = value.astype(jnp.bfloat16)
    return high, (value - high.astype(jnp.float32)).astype(jnp.bfloat16)


def weight_kernel(own, cross, chip, feat0, feat1, feat32, give, keep0, keep3, term):
    blocks, channels, edge = keep0.shape
    held = []
    for k, (feat, at) in enumerate(((feat0, 0), (feat1, 0), (feat32, blocks), (feat32, 0))):
        for b in range(blocks):
            i = k * blocks + b
            g = own[i] + cross[i].astype(jnp.float32) + chip[i].astype(jnp.float32)
            if k == 0:
                keep0[b] = g
            elif k == 3:
                keep3[b] = g
            else:
                give[(k - 1) * blocks + b] = g.astype(jnp.bfloat16)
            held.append((g, feat, (at + b) * edge))
    acc = None
    for (g, feat, at), (g2, feat2, at2) in zip(held[::2], held[1::2]):
        rows = jnp.concatenate([feat[pl.ds(at, edge), :], feat2[pl.ds(at2, edge), :]], axis=0)
        for piece in split(jnp.concatenate([g, g2], axis=1)):
            prod = jnp.dot(piece, rows, preferred_element_type=jnp.float32)
            acc = prod if acc is None else acc + prod
    acc = acc.T
    parts, both, _ = term.shape
    height = acc.shape[0] // parts
    for i in range(parts):
        halves = [
            acc[i * height : (i + 1) * height, j * edge : (j + 1) * edge]
            for j in range(both // height)
        ]
        term[i] = jnp.concatenate(halves, axis=0).astype(term.dtype)


def sum_kernel(scale, got, total):
    acc = got[0].astype(jnp.float32)
    for i in range(1, got.shape[0]):
        acc = acc + got[i].astype(jnp.float32)
    total[...] = acc / scale


def sum_of(got, scale):
    return pl.pallas_call(
        functools.partial(sum_kernel, scale),
        out_shape=jax.ShapeDtypeStruct(got.shape[1:], jnp.float32),
        in_specs=[VMEM],
        out_specs=VMEM,
        compiler_params=pltpu.CompilerParams(vmem_limit_bytes=16 << 20),
        name="piece_sum",
    )(got)


def spread_kernel(got, copies):
    acc = got[0].astype(jnp.float32)
    for i in range(1, got.shape[0]):
        acc = acc + got[i].astype(jnp.float32)
    value = acc.astype(copies.dtype)
    for i in range(copies.shape[0]):
        copies[i] = value


def spread_pair_kernel(mine, other, copies):
    value = (mine[...] + other[...]).astype(copies.dtype)
    for i in range(copies.shape[0]):
        copies[i] = value


def spread(kernel, count, shape, *parts):
    return pl.pallas_call(
        kernel,
        out_shape=jax.ShapeDtypeStruct((count,) + shape, jnp.bfloat16),
        in_specs=[VMEM] * len(parts),
        out_specs=VMEM,
        compiler_params=pltpu.CompilerParams(vmem_limit_bytes=16 << 20),
        name="spread",
    )(*parts)


def feature_kernel(keep, pair, other, weight, grad):
    blocks, _, edge = keep.shape
    for b in range(blocks):
        g = keep[b] + pair[b].astype(jnp.float32) + other[b].astype(jnp.float32)
        acc = None
        for piece in split(g.T):
            prod = lax.dot_general(
                piece, weight[...], (((1,), (1,)), ((), ())), preferred_element_type=jnp.float32
            )
            acc = prod if acc is None else acc + prod
        grad[pl.ds(b * edge, edge), :] = acc


def hops(cols, flips):
    return [(c * cols + i, c * cols + (i ^ flip)) for c, flip in enumerate(flips) for i in range(cols)]


def swap(array, axes, count, first):
    pairs = [(i, i + 1) for i in range(first, count - 1, 2)]
    return lax.ppermute(array, axes, pairs + [(j, i) for i, j in pairs])


def local(features, pre_act, upstream, weight, tile_values, tile_list, tile_counts, *, sizes):
    y, z, x = sizes
    rows = y * z * 2
    rows_dev, channels = features.shape
    slot_count, edge = tile_values.shape[:2]
    blocks = rows_dev // edge
    width = x * blocks
    params = pltpu.CompilerParams(vmem_limit_bytes=40 << 20)
    held = [
        pltpu.with_memory_space_constraint(a, pltpu.HBM)
        for a in (tile_list.T, pre_act, upstream, tile_values)
    ]
    cross, chip, own = pl.pallas_call(
        tile_kernel,
        out_shape=(
            jax.ShapeDtypeStruct((width, channels, edge), jnp.bfloat16),
            jax.ShapeDtypeStruct((width, channels, edge), jnp.bfloat16),
            jax.ShapeDtypeStruct((width, channels, edge), jnp.float32),
        ),
        in_specs=[SMEM] + [HBM] * 4,
        out_specs=(VMEM,) * 3,
        scratch_shapes=[
            pltpu.SMEM((3, slot_count), jnp.int32),
            pltpu.VMEM((rows_dev, channels), jnp.bfloat16),
            pltpu.VMEM((rows_dev, channels), jnp.float32),
            pltpu.VMEM((slot_count, edge, edge), jnp.bfloat16),
            pltpu.VMEM((blocks, channels, edge), jnp.bfloat16),
            pltpu.VMEM((3 * width, channels, edge), jnp.float32),
            pltpu.SemaphoreType.DMA((4,)),
        ],
        compiler_params=params,
        name="tile_sums",
    )(tile_counts, *held)
    near, far = hops(x, (1, 3)), hops(x, (3, 1))
    feat1 = lax.ppermute(features, ("core", "x"), near)
    chip, feat1 = lax.optimization_barrier((chip, feat1))
    from_cross = swap(cross, ("y", "z", "core"), rows, 1)
    from_chip = swap(chip, "core", 2, 0)
    feat32 = lax.ppermute(jnp.concatenate([features, feat1], axis=0), ("core", "x"), far)
    halves = channels // edge
    height = channels // (x * y)
    third = (blocks, channels, edge)
    give, keep0, keep3, term = pl.pallas_call(
        weight_kernel,
        out_shape=(
            jax.ShapeDtypeStruct((2 * blocks, channels, edge), jnp.bfloat16),
            jax.ShapeDtypeStruct(third, jnp.float32),
            jax.ShapeDtypeStruct(third, jnp.float32),
            jax.ShapeDtypeStruct((x * y, halves * height, edge), jnp.bfloat16),
        ),
        in_specs=[VMEM] * 6,
        out_specs=(VMEM,) * 4,
        compiler_params=params,
        name="weight_term",
    )(own, from_cross, from_chip, features, feat1, feat32)
    from_near = lax.ppermute(give, ("core", "x"), near)
    onward = (keep3 + from_near[blocks:].astype(jnp.float32)).astype(jnp.bfloat16)
    from_far = lax.ppermute(onward, ("core", "x"), far)
    grad_features = pl.pallas_call(
        feature_kernel,
        out_shape=jax.ShapeDtypeStruct((rows_dev, channels), jnp.float32),
        in_specs=[VMEM] * 4,
        out_specs=VMEM,
        compiler_params=params,
        name="feature_grad",
    )(keep0, from_near, from_far, weight)
    got = lax.all_to_all(term, ("x", "y"), 0, 0)
    mine = sum_of(got, math.sqrt(rows * x * rows_dev))
    other = swap(mine, "core", 2, 0)
    copies = spread(spread_pair_kernel, z, mine.shape, mine, other)
    got = lax.all_to_all(copies, "z", 0, 0)
    copies = spread(spread_kernel, x * y, mine.shape, got)
    pieces = lax.all_to_all(copies, ("x", "y"), 0, 0).astype(jnp.float32)
    pieces = pieces.reshape(x * y, halves, height, edge)
    grad_weight = pieces.transpose(0, 2, 1, 3).reshape(channels, channels)
    return (grad_features, grad_weight)


def solution(mesh):
    rows, x = mesh.devices.shape
    y = math.gcd(rows, 8)
    z = rows // y // 2
    every = ("y", "z", "core", "x")
    fine = Mesh(mesh.devices.reshape(y, z, 2, x), every)
    return jax.shard_map(
        functools.partial(local, sizes=(y, z, x)),
        mesh=fine,
        in_specs=(
            P(every, None),
            P(every, None),
            P(every, None),
            P(),
            P(every, None, None),
            P(every, None),
            P(every),
        ),
        out_specs=(P(every, None), P()),
        check_vma=False,
    )
```

```python
import functools
import math

import jax
import jax.numpy as jnp
from jax import lax
from jax.experimental import pallas as pl
from jax.experimental.pallas import tpu as pltpu
from jax.sharding import Mesh, PartitionSpec as P

GROUP = 24
VMEM = pl.BlockSpec(memory_space=pltpu.VMEM)
SMEM = pl.BlockSpec(memory_space=pltpu.SMEM)
HBM = pl.BlockSpec(memory_space=pltpu.HBM)


def tile_kernel(
    count, slots_hbm, pre_hbm, up_hbm, tiles_hbm,
    cross, chip, own,
    slots, pre, up, tiles, masked_t, total, arrived,
):
    pairs = ((slots_hbm, slots), (up_hbm, up), (pre_hbm, pre), (tiles_hbm, tiles))
    copies = [pltpu.make_async_copy(a, b, arrived.at[i]) for i, (a, b) in enumerate(pairs)]
    for copy in copies:
        copy.start()
    total[...] = jnp.zeros_like(total)
    blocks, _, edge = masked_t.shape
    width = own.shape[0]
    copies[1].wait()
    copies[2].wait()
    for d in range(blocks):
        rows = pl.ds(d * edge, edge)
        kept = jnp.where(pre[rows, :].astype(jnp.float32) > 0, up[rows, :], 0.0)
        masked_t[d] = kept.T.astype(jnp.bfloat16)
    copies[0].wait()
    copies[3].wait()
    live = count[0]
    row = slots[0, 0] // width
    first = (row - 1) * width

    def body(group, carry):
        for u in range(GROUP):
            slot = group * GROUP + u
            dst = slots[0, slot] % blocks
            src = slots[1, slot] - first
            tile = tiles[slots[2, slot]]
            tile = jnp.where(slot < live, tile, jnp.zeros_like(tile))
            total[src] += jnp.dot(masked_t[dst], tile, preferred_element_type=jnp.float32)
        return carry

    lax.fori_loop(0, (live + GROUP - 1) // GROUP, body, 0)
    core = row % 2
    cols = width // blocks
    col = slots[0, 0] // blocks % cols
    for k in range(cols):
        to = pl.ds(k * blocks, blocks)
        ahead, back = (k ^ col) * blocks, ((cols - k) % cols ^ col) * blocks
        mine, other = jnp.where(core == 0, ahead, back), jnp.where(core == 0, back, ahead)
        cross[to] = total[pl.ds(2 * core * width + other, blocks)].astype(jnp.bfloat16)
        chip[to] = total[pl.ds(2 * (1 - core) * width + other, blocks)].astype(jnp.bfloat16)
        own[to] = total[pl.ds(width + mine, blocks)]


def split(value):
    high = value.astype(jnp.bfloat16)
    return high, (value - high.astype(jnp.float32)).astype(jnp.bfloat16)


def weight_kernel(own, cross, chip, feat0, feat1, feat32, give1, give2, keep0, keep3, term):
    blocks, channels, edge = keep0.shape
    held = []
    for k, (feat, at) in enumerate(((feat0, 0), (feat1, 0), (feat32, blocks), (feat32, 0))):
        for b in range(blocks):
            i = k * blocks + b
            g = own[i] + cross[i].astype(jnp.float32) + chip[i].astype(jnp.float32)
            if k == 0:
                keep0[b] = g
            elif k == 3:
                keep3[b] = g
            else:
                (give1 if k == 1 else give2)[b] = g.astype(jnp.bfloat16)
            held.append((g, feat, (at + b) * edge))
    acc = None
    for (g, feat, at), (g2, feat2, at2) in zip(held[::2], held[1::2]):
        rows = jnp.concatenate([feat[pl.ds(at, edge), :], feat2[pl.ds(at2, edge), :]], axis=0)
        for piece in split(jnp.concatenate([g, g2], axis=1)):
            prod = jnp.dot(piece, rows, preferred_element_type=jnp.float32)
            acc = prod if acc is None else acc + prod
    acc = acc.T
    parts, both, _ = term.shape
    height = acc.shape[0] // parts
    for i in range(parts):
        halves = [
            acc[i * height : (i + 1) * height, j * edge : (j + 1) * edge]
            for j in range(both // height)
        ]
        term[i] = jnp.concatenate(halves, axis=0).astype(term.dtype)


def spread_kernel(scale, got, copies):
    acc = got[0].astype(jnp.float32)
    for i in range(1, got.shape[0]):
        acc = acc + got[i].astype(jnp.float32)
    value = (acc / scale).astype(copies.dtype)
    for i in range(copies.shape[0]):
        copies[i] = value


def spread(got, count, scale):
    return pl.pallas_call(
        functools.partial(spread_kernel, scale),
        out_shape=jax.ShapeDtypeStruct((count,) + got.shape[1:], jnp.bfloat16),
        in_specs=[VMEM],
        out_specs=VMEM,
        compiler_params=pltpu.CompilerParams(vmem_limit_bytes=16 << 20),
        name="spread",
    )(got)


def feature_kernel(keep, pair, other, weight, grad):
    blocks, _, edge = keep.shape
    for b in range(blocks):
        g = keep[b] + pair[b].astype(jnp.float32) + other[b].astype(jnp.float32)
        acc = None
        for piece in split(g.T):
            prod = lax.dot_general(
                piece, weight[...], (((1,), (1,)), ((), ())), preferred_element_type=jnp.float32
            )
            acc = prod if acc is None else acc + prod
        grad[pl.ds(b * edge, edge), :] = acc


def hops(cols, flips):
    return [(c * cols + i, c * cols + (i ^ flip)) for c, flip in enumerate(flips) for i in range(cols)]


def swap(array, axes, count, first):
    pairs = [(i, i + 1) for i in range(first, count - 1, 2)]
    return lax.ppermute(array, axes, pairs + [(j, i) for i, j in pairs])


def local(features, pre_act, upstream, weight, tile_values, tile_list, tile_counts, *, sizes):
    y, z, x = sizes
    rows = y * z * 2
    rows_dev, channels = features.shape
    slot_count, edge = tile_values.shape[:2]
    blocks = rows_dev // edge
    width = x * blocks
    params = pltpu.CompilerParams(vmem_limit_bytes=40 << 20)
    held = [
        pltpu.with_memory_space_constraint(a, pltpu.HBM)
        for a in (tile_list.T, pre_act, upstream, tile_values)
    ]
    cross, chip, own = pl.pallas_call(
        tile_kernel,
        out_shape=(
            jax.ShapeDtypeStruct((width, channels, edge), jnp.bfloat16),
            jax.ShapeDtypeStruct((width, channels, edge), jnp.bfloat16),
            jax.ShapeDtypeStruct((width, channels, edge), jnp.float32),
        ),
        in_specs=[SMEM] + [HBM] * 4,
        out_specs=(VMEM,) * 3,
        scratch_shapes=[
            pltpu.SMEM((3, slot_count), jnp.int32),
            pltpu.VMEM((rows_dev, channels), jnp.bfloat16),
            pltpu.VMEM((rows_dev, channels), jnp.float32),
            pltpu.VMEM((slot_count, edge, edge), jnp.bfloat16),
            pltpu.VMEM((blocks, channels, edge), jnp.bfloat16),
            pltpu.VMEM((3 * width, channels, edge), jnp.float32),
            pltpu.SemaphoreType.DMA((4,)),
        ],
        compiler_params=params,
        name="tile_sums",
    )(tile_counts, *held)
    near, far = hops(x, (1, 3)), hops(x, (3, 1))
    feat1 = lax.ppermute(features, ("core", "x"), near)
    chip, feat1 = lax.optimization_barrier((chip, feat1))
    from_cross = swap(cross, ("y", "z", "core"), rows, 1)
    from_chip = swap(chip, "core", 2, 0)
    feat32 = lax.ppermute(jnp.concatenate([features, feat1], axis=0), ("core", "x"), far)
    halves = channels // edge
    height = channels // (x * y)
    third = (blocks, channels, edge)
    give1, give2, keep0, keep3, term = pl.pallas_call(
        weight_kernel,
        out_shape=(
            jax.ShapeDtypeStruct(third, jnp.bfloat16),
            jax.ShapeDtypeStruct(third, jnp.bfloat16),
            jax.ShapeDtypeStruct(third, jnp.float32),
            jax.ShapeDtypeStruct(third, jnp.float32),
            jax.ShapeDtypeStruct((x * y, halves * height, edge), jnp.bfloat16),
        ),
        in_specs=[VMEM] * 6,
        out_specs=(VMEM,) * 5,
        compiler_params=params,
        name="weight_term",
    )(own, from_cross, from_chip, features, feat1, feat32)
    passing = lax.ppermute(give2, ("core", "x"), near)
    onward = (keep3 + passing.astype(jnp.float32)).astype(jnp.bfloat16)
    from_far = lax.ppermute(onward, ("core", "x"), far)
    got = lax.all_to_all(term, ("x", "y"), 0, 0)
    got, give1 = lax.optimization_barrier((got, give1))
    from_near = lax.ppermute(give1, ("core", "x"), near)
    copies = spread(got, 2 * z, math.sqrt(rows * x * rows_dev))
    got = lax.all_to_all(copies, ("z", "core"), 0, 0)
    got, from_near, from_far = lax.optimization_barrier((got, from_near, from_far))
    grad_features = pl.pallas_call(
        feature_kernel,
        out_shape=jax.ShapeDtypeStruct((rows_dev, channels), jnp.float32),
        in_specs=[VMEM] * 4,
        out_specs=VMEM,
        compiler_params=params,
        name="feature_grad",
    )(keep0, from_near, from_far, weight)
    copies = spread(got, x * y, 1.0)
    pieces = lax.all_to_all(copies, ("x", "y"), 0, 0).astype(jnp.float32)
    pieces = pieces.reshape(x * y, halves, height, edge)
    grad_weight = pieces.transpose(0, 2, 1, 3).reshape(channels, channels)
    return (grad_features, grad_weight)


def solution(mesh):
    rows, x = mesh.devices.shape
    y = math.gcd(rows, 8)
    z = rows // y // 2
    every = ("y", "z", "core", "x")
    fine = Mesh(mesh.devices.reshape(y, z, 2, x), every)
    return jax.shard_map(
        functools.partial(local, sizes=(y, z, x)),
        mesh=fine,
        in_specs=(
            P(every, None),
            P(every, None),
            P(every, None),
            P(),
            P(every, None, None),
            P(every, None),
            P(every),
        ),
        out_specs=(P(every, None), P()),
        check_vma=False,
    )
```

```python
import functools
import math

import jax
import jax.numpy as jnp
from jax import lax
from jax.experimental import pallas as pl
from jax.experimental.pallas import tpu as pltpu
from jax.sharding import Mesh, PartitionSpec as P

GROUP = 24
VMEM = pl.BlockSpec(memory_space=pltpu.VMEM)
SMEM = pl.BlockSpec(memory_space=pltpu.SMEM)
HBM = pl.BlockSpec(memory_space=pltpu.HBM)


def tile_kernel(
    count, slots_hbm, pre_hbm, up_hbm, tiles_hbm,
    cross, chip, own,
    slots, pre, up, tiles, masked_t, total, arrived,
):
    pairs = ((slots_hbm, slots), (up_hbm, up), (pre_hbm, pre), (tiles_hbm, tiles))
    copies = [pltpu.make_async_copy(a, b, arrived.at[i]) for i, (a, b) in enumerate(pairs)]
    for copy in copies:
        copy.start()
    total[...] = jnp.zeros_like(total)
    blocks, _, edge = masked_t.shape
    width = own.shape[0]
    copies[1].wait()
    copies[2].wait()
    for d in range(blocks):
        rows = pl.ds(d * edge, edge)
        kept = jnp.where(pre[rows, :].astype(jnp.float32) > 0, up[rows, :], 0.0)
        masked_t[d] = kept.T.astype(jnp.bfloat16)
    copies[0].wait()
    copies[3].wait()
    live = count[0]
    row = slots[0, 0] // width
    first = (row - 1) * width

    def body(group, carry):
        for u in range(GROUP):
            slot = group * GROUP + u
            dst = slots[0, slot] % blocks
            src = slots[1, slot] - first
            tile = tiles[slots[2, slot]]
            tile = jnp.where(slot < live, tile, jnp.zeros_like(tile))
            total[src] += jnp.dot(masked_t[dst], tile, preferred_element_type=jnp.float32)
        return carry

    lax.fori_loop(0, (live + GROUP - 1) // GROUP, body, 0)
    core = row % 2
    cols = width // blocks
    col = slots[0, 0] // blocks % cols
    for k in range(cols):
        to = pl.ds(k * blocks, blocks)
        ahead, back = (k ^ col) * blocks, ((cols - k) % cols ^ col) * blocks
        mine, other = jnp.where(core == 0, ahead, back), jnp.where(core == 0, back, ahead)
        cross[to] = total[pl.ds(2 * core * width + other, blocks)].astype(jnp.bfloat16)
        chip[to] = total[pl.ds(2 * (1 - core) * width + other, blocks)].astype(jnp.bfloat16)
        own[to] = total[pl.ds(width + mine, blocks)]


def split(value):
    high = value.astype(jnp.bfloat16)
    return high, (value - high.astype(jnp.float32)).astype(jnp.bfloat16)


def weight_kernel(own, cross, chip, feat0, feat1, feat32, give1, give2, keep0, keep3, term):
    blocks, channels, edge = keep0.shape
    held = []
    for k, (feat, at) in enumerate(((feat0, 0), (feat1, 0), (feat32, blocks), (feat32, 0))):
        for b in range(blocks):
            i = k * blocks + b
            g = own[i] + cross[i].astype(jnp.float32) + chip[i].astype(jnp.float32)
            if k == 0:
                keep0[b] = g
            elif k == 3:
                keep3[b] = g
            else:
                (give1 if k == 1 else give2)[b] = g.astype(jnp.bfloat16)
            held.append((g, feat, (at + b) * edge))
    acc = None
    for (g, feat, at), (g2, feat2, at2) in zip(held[::2], held[1::2]):
        rows = jnp.concatenate([feat[pl.ds(at, edge), :], feat2[pl.ds(at2, edge), :]], axis=0)
        for piece in split(jnp.concatenate([g, g2], axis=1)):
            prod = jnp.dot(piece, rows, preferred_element_type=jnp.float32)
            acc = prod if acc is None else acc + prod
    acc = acc.T
    parts, both, _ = term.shape
    height = acc.shape[0] // parts
    for i in range(parts):
        halves = [
            acc[i * height : (i + 1) * height, j * edge : (j + 1) * edge]
            for j in range(both // height)
        ]
        term[i] = jnp.concatenate(halves, axis=0).astype(term.dtype)


def spread_kernel(scale, got, copies):
    acc = got[0].astype(jnp.float32)
    for i in range(1, got.shape[0]):
        acc = acc + got[i].astype(jnp.float32)
    value = (acc / scale).astype(copies.dtype)
    for i in range(copies.shape[0]):
        copies[i] = value


def spread(got, count, scale):
    return pl.pallas_call(
        functools.partial(spread_kernel, scale),
        out_shape=jax.ShapeDtypeStruct((count,) + got.shape[1:], jnp.bfloat16),
        in_specs=[VMEM],
        out_specs=VMEM,
        compiler_params=pltpu.CompilerParams(vmem_limit_bytes=16 << 20),
        name="spread",
    )(got)


def feature_kernel(keep, pair, other, weight, grad):
    blocks, _, edge = keep.shape
    for b in range(blocks):
        g = keep[b] + pair[b].astype(jnp.float32) + other[b].astype(jnp.float32)
        acc = None
        for piece in split(g.T):
            prod = lax.dot_general(
                piece, weight[...], (((1,), (1,)), ((), ())), preferred_element_type=jnp.float32
            )
            acc = prod if acc is None else acc + prod
        grad[pl.ds(b * edge, edge), :] = acc


def hops(cols, flips):
    return [(c * cols + i, c * cols + (i ^ flip)) for c, flip in enumerate(flips) for i in range(cols)]


def swap(array, axes, count, first):
    pairs = [(i, i + 1) for i in range(first, count - 1, 2)]
    return lax.ppermute(array, axes, pairs + [(j, i) for i, j in pairs])


def local(features, pre_act, upstream, weight, tile_values, tile_list, tile_counts, *, sizes):
    y, z, x = sizes
    rows = y * z * 2
    rows_dev, channels = features.shape
    slot_count, edge = tile_values.shape[:2]
    blocks = rows_dev // edge
    width = x * blocks
    params = pltpu.CompilerParams(vmem_limit_bytes=40 << 20)
    held = [
        pltpu.with_memory_space_constraint(a, pltpu.HBM)
        for a in (tile_list.T, pre_act, upstream, tile_values)
    ]
    cross, chip, own = pl.pallas_call(
        tile_kernel,
        out_shape=(
            jax.ShapeDtypeStruct((width, channels, edge), jnp.bfloat16),
            jax.ShapeDtypeStruct((width, channels, edge), jnp.bfloat16),
            jax.ShapeDtypeStruct((width, channels, edge), jnp.float32),
        ),
        in_specs=[SMEM] + [HBM] * 4,
        out_specs=(VMEM,) * 3,
        scratch_shapes=[
            pltpu.SMEM((3, slot_count), jnp.int32),
            pltpu.VMEM((rows_dev, channels), jnp.bfloat16),
            pltpu.VMEM((rows_dev, channels), jnp.float32),
            pltpu.VMEM((slot_count, edge, edge), jnp.bfloat16),
            pltpu.VMEM((blocks, channels, edge), jnp.bfloat16),
            pltpu.VMEM((3 * width, channels, edge), jnp.float32),
            pltpu.SemaphoreType.DMA((4,)),
        ],
        compiler_params=params,
        name="tile_sums",
    )(tile_counts, *held)
    near, far = hops(x, (1, 3)), hops(x, (3, 1))
    feat1 = lax.ppermute(features, ("core", "x"), near)
    chip, feat1 = lax.optimization_barrier((chip, feat1))
    from_cross = swap(cross, ("y", "z", "core"), rows, 1)
    from_chip = swap(chip, "core", 2, 0)
    feat32 = lax.ppermute(jnp.concatenate([features, feat1], axis=0), ("core", "x"), far)
    halves = channels // edge
    height = channels // (x * y)
    third = (blocks, channels, edge)
    give1, give2, keep0, keep3, term = pl.pallas_call(
        weight_kernel,
        out_shape=(
            jax.ShapeDtypeStruct(third, jnp.bfloat16),
            jax.ShapeDtypeStruct(third, jnp.bfloat16),
            jax.ShapeDtypeStruct(third, jnp.float32),
            jax.ShapeDtypeStruct(third, jnp.float32),
            jax.ShapeDtypeStruct((x * y, halves * height, edge), jnp.bfloat16),
        ),
        in_specs=[VMEM] * 6,
        out_specs=(VMEM,) * 5,
        compiler_params=params,
        name="weight_term",
    )(own, from_cross, from_chip, features, feat1, feat32)
    passing = lax.ppermute(give2, ("core", "x"), near)
    from_near = lax.ppermute(give1, ("core", "x"), near)
    onward = (keep3 + passing.astype(jnp.float32)).astype(jnp.bfloat16)
    from_far = lax.ppermute(onward, ("core", "x"), far)
    got = lax.all_to_all(term, ("x", "y"), 0, 0)
    copies = spread(got, 2 * z, math.sqrt(rows * x * rows_dev))
    got = lax.all_to_all(copies, ("z", "core"), 0, 0)
    got, from_near, from_far = lax.optimization_barrier((got, from_near, from_far))
    grad_features = pl.pallas_call(
        feature_kernel,
        out_shape=jax.ShapeDtypeStruct((rows_dev, channels), jnp.float32),
        in_specs=[VMEM] * 4,
        out_specs=VMEM,
        compiler_params=params,
        name="feature_grad",
    )(keep0, from_near, from_far, weight)
    copies = spread(got, x * y, 1.0)
    pieces = lax.all_to_all(copies, ("x", "y"), 0, 0).astype(jnp.float32)
    pieces = pieces.reshape(x * y, halves, height, edge)
    grad_weight = pieces.transpose(0, 2, 1, 3).reshape(channels, channels)
    return (grad_features, grad_weight)


def solution(mesh):
    rows, x = mesh.devices.shape
    y = math.gcd(rows, 8)
    z = rows // y // 2
    every = ("y", "z", "core", "x")
    fine = Mesh(mesh.devices.reshape(y, z, 2, x), every)
    return jax.shard_map(
        functools.partial(local, sizes=(y, z, x)),
        mesh=fine,
        in_specs=(
            P(every, None),
            P(every, None),
            P(every, None),
            P(),
            P(every, None, None),
            P(every, None),
            P(every),
        ),
        out_specs=(P(every, None), P()),
        check_vma=False,
    )
```
